32 devices in a mesh: dp: 4 (over z), expert: 8 (over y, x, core).
Axes of the slice: x: 2, y: 2, z: 4, core: 2. Of those that a mesh axis runs over, the one named last changes fastest.
Arguments:
- tokens: bfloat16 [4096, 2048], P(('dp', 'expert')), may hold values from -6 to 6
- expert_ids: int32 [4096, 2], P(('dp', 'expert')), may hold values from 0 to 7, as said below
- slot_index: int32 [4096, 2], P(('dp', 'expert')), may hold values from 0 to 63, as said below
- routing_gates: float32 [4096, 2], P(('dp', 'expert')), may hold values from 0.2 to 1
- grad_out: bfloat16 [4096, 2048], P(('dp', 'expert')), may hold values from -1.5 to 1.5
- w_gate: bfloat16 [8, 2048, 768], P('expert', 'dp'), may hold values from -0.125 to 0.125
- w_up: bfloat16 [8, 2048, 768], P('expert', 'dp'), may hold values from -0.125 to 0.125
- w_down: bfloat16 [8, 2048, 768], P('expert', 'dp'), may hold values from -0.21875 to 0.21875
Outputs:
- layer_out: bfloat16 [4096, 2048], P(('dp', 'expert'))
- grad_tokens: bfloat16 [4096, 2048], P(('dp', 'expert'))
- grad_gates: float32 [4096, 2], P(('dp', 'expert'))
- grad_w_gate: bfloat16 [8, 2048, 768], P('expert', 'dp')
- grad_w_up: bfloat16 [8, 2048, 768], P('expert', 'dp')
- grad_w_down: bfloat16 [8, 2048, 768], P('expert', 'dp')
The draws below stay inside these ranges and needn't reach their ends.
Inputs may be any that keep to these rules, and one draw needn't show every extreme that they name: `expert_ids`: each row names 2 different experts. In each aligned block of 128 rows no expert is named more than 64 times; for each group of 8 blocks in a row, some expert is named exactly 64 times in every block of the group. `slot_index`: within one aligned block of 128 rows, the pairs that name one expert have distinct places, 0 up to their number minus one.
All inputs are finite; a program needn't handle non-finite values.
Results may differ from the reference program's by a relative error of at most 0.014.
Values may be sent and summed in bfloat16 or wider, within the bound.
No kernel may reach another device: no remote copies, remote signals or barrier semaphores. Data moves between devices by JAX's collectives and lax.ppermute only.
A program may use at most 128 MiB of HBM per device.

```python
import jax
import jax.numpy as jnp
from jax import lax

D = 2048
FFN = 768
TOPK = 2
TOK_DEV = 128
EXPERTS = 8
CAP = 64
TOKENS = 4096


def routing(key):
    block_count = TOKENS // TOK_DEV
    average = TOK_DEV * TOPK // EXPERTS
    half_count = EXPERTS // 2
    position = jnp.arange(TOK_DEV * TOPK, dtype=jnp.int32)

    def one_block(block_index):
        block_key = jax.random.fold_in(key, block_index)
        key_shift, key_label, key_order = jax.random.split(block_key, 3)
        offsets = jax.random.randint(key_shift, (half_count,), -average, average + 1, dtype=jnp.int32)
        offsets = offsets.at[0].set(average)
        counts = jnp.concatenate([average + offsets, average - offsets])
        run_ends = jnp.cumsum(counts)
        starts = run_ends - counts
        run_index = jnp.sum((position[:, None] >= run_ends[None, :]).astype(jnp.int32), axis=1)
        slot_value = position - starts[run_index]
        group_key = jax.random.fold_in(key, block_count + block_index // EXPERTS)
        full_expert = jax.random.randint(group_key, (), 0, EXPERTS, dtype=jnp.int32)
        labels = jax.random.permutation(key_label, EXPERTS).astype(jnp.int32)
        labels = jnp.where(labels == full_expert, labels[0], labels).at[0].set(full_expert)
        expert_value = labels[run_index]
        token_order = jax.random.permutation(key_order, TOK_DEV).astype(jnp.int32)
        row_index = token_order[position % TOK_DEV]
        column_index = position // TOK_DEV
        expert_table = jnp.zeros((TOK_DEV, TOPK), jnp.int32).at[row_index, column_index].set(expert_value)
        slot_table = jnp.zeros((TOK_DEV, TOPK), jnp.int32).at[row_index, column_index].set(slot_value)
        return (expert_table, slot_table)
    expert_tables, slot_tables = jax.vmap(one_block)(jnp.arange(block_count, dtype=jnp.int32))
    return (expert_tables.reshape(TOKENS, TOPK), slot_tables.reshape(TOKENS, TOPK))


def draw_expert_ids(key, part):
    return routing(jax.random.fold_in(key, 11))[0]


def draw_slot_index(key, part):
    return routing(jax.random.fold_in(key, 11))[1]


def with_spikes(array, own_key, source, target, shards_of, factor):
    owner, partner = [(jnp.arange(array.shape[dim]) // (array.shape[dim] // shards_of)).reshape([-1 if axis == dim else 1 for axis in range(array.ndim)]) for dim in (source, target)]
    chosen = jax.random.permutation(own_key, shards_of)[partner]
    strong = (owner == chosen) | (owner == (partner + shards_of // 2) % shards_of)
    return jnp.where(strong, factor * array, array)


def block_levels(key, shape, shards, low, largest):
    def one(dim, shards_of):
        heights = jax.random.uniform(jax.random.fold_in(jax.random.fold_in(key, 6), dim), (shards_of,), jnp.float32, low / len(shards), largest / len(shards))
        return jnp.repeat(jnp.exp(heights), shape[dim] // shards_of).reshape((-1,) + (1,) * (len(shape) - dim - 1))

    level = one(*shards[0])
    for cut in shards[1:]:
        level = level * one(*cut)
    return level


def gaussian(key, extent, scale, reach, pieces=(), kind=jnp.bfloat16):
    level = block_levels(key, extent, pieces, -0.22, 0.18) if pieces else 1.0
    drawn = jax.random.normal(key, extent, jnp.float32) * scale * level
    return jnp.minimum(jnp.maximum(drawn, -reach), reach).astype(kind)


def gaussian_with(stream_key, shape, spread, limit, cuts, heavy, kind=jnp.bfloat16):
    values = spread * jax.random.normal(stream_key, shape, jnp.float32)
    if cuts:
        values = values * block_levels(stream_key, shape, cuts, -0.22, 0.18)
    return jnp.clip(with_spikes(values, jax.random.fold_in(stream_key, 3), *heavy), -limit, limit).astype(kind)


def setup_inputs(seed: int = 0) -> dict:
    arg_keys = jax.random.split(jax.random.key(seed), 9)
    return {
        "tokens": gaussian_with(arg_keys[0], (TOKENS, D), 1.0, 6.0, ((0, 32),), (0, 1, 32, 2.75)),
        "expert_ids": draw_expert_ids(jax.random.fold_in(arg_keys[8], 71), 0),
        "slot_index": draw_slot_index(jax.random.fold_in(arg_keys[8], 71), 0),
        "routing_gates": jnp.clip(0.2 + 0.8 * jax.random.uniform(arg_keys[3], (TOKENS, TOPK), jnp.float32) ** block_levels(arg_keys[3], (TOKENS, TOPK), ((0, 32),), -0.2, 0.2), 0.2, 1.0),
        "grad_out": gaussian(arg_keys[4], (TOKENS, D), 0.25, 1.5, ((0, 32),)),
        "w_gate": gaussian(arg_keys[5], (EXPERTS, D, FFN), D ** -0.5, 0.125, ((0, 8), (1, 4))),
        "w_up": gaussian(arg_keys[6], (EXPERTS, D, FFN), D ** -0.5, 0.125, ((0, 8), (1, 4))),
        "w_down": gaussian(arg_keys[7], (EXPERTS, D, FFN), FFN ** -0.5, 0.21875, ((0, 8), (1, 4))),
    }


def group_gradient(left_rows, right_rows, group_count):
    left_groups = left_rows.reshape(group_count, -1, left_rows.shape[1]).astype(jnp.float32)
    right_groups = right_rows.reshape(group_count, -1, right_rows.shape[1]).astype(jnp.float32)
    partial_sums = jnp.einsum("grd,grf->gdf", left_groups, right_groups, precision=lax.Precision.HIGHEST)
    rounded = lax.optimization_barrier(partial_sums.astype(jnp.bfloat16))
    return jnp.sum(rounded.astype(jnp.float32), axis=0).astype(jnp.bfloat16)


def reference(tokens, expert_ids, slot_index, routing_gates, grad_out, w_gate, w_up, w_down):
    block_count = TOKENS // TOK_DEV
    group_count = block_count // EXPERTS
    pair_count = TOK_DEV * TOPK
    tok_blocks = tokens.reshape(block_count, TOK_DEV, D)
    grad_blocks = grad_out.reshape(block_count, TOK_DEV, D)
    gate_blocks = routing_gates.reshape(block_count, pair_count)
    target = (expert_ids * CAP + slot_index).reshape(block_count, pair_count).astype(jnp.int32)
    pair_index = jnp.arange(pair_count, dtype=jnp.int32)

    def invert(row_target):
        return jnp.full((EXPERTS * CAP,), -1, jnp.int32).at[row_target].set(pair_index)

    source = jax.vmap(invert)(target)
    block_index = jnp.arange(block_count, dtype=jnp.int32)[:, None]
    flat_block = jnp.broadcast_to(block_index, (block_count, CAP)).reshape(-1)

    def per_expert(totals, expert):
        out_sum, back_sum, gate_grad = totals
        chosen = lax.dynamic_slice_in_dim(source, expert * CAP, CAP, 1)
        occupied = chosen >= 0
        pair_safe = jnp.where(occupied, chosen, 0).astype(jnp.int32)
        token_safe = (pair_safe // TOPK).astype(jnp.int32)
        live_float = jnp.where(occupied, 1.0, 0.0).astype(jnp.float32).reshape(-1)
        zero_row = jnp.zeros((), jnp.bfloat16)
        rows_in = jnp.where(occupied[..., None], tok_blocks[block_index, token_safe], zero_row)
        grad_rows_raw = grad_blocks[block_index, token_safe]
        gate_value = gate_blocks[block_index, pair_safe].reshape(-1) * live_float
        flat_in = rows_in.reshape(-1, D)
        flat_grad_raw = grad_rows_raw.reshape(-1, D)
        flat_grad = (gate_value[:, None] * flat_grad_raw.astype(jnp.float32)).astype(jnp.bfloat16)
        gate_matrix = w_gate[expert]
        up_matrix = w_up[expert]
        down_matrix = w_down[expert]
        gate_pre = jnp.dot(flat_in, gate_matrix, preferred_element_type=jnp.float32)
        up_pre = jnp.dot(flat_in, up_matrix, preferred_element_type=jnp.float32)
        sigmoid_gate = jax.nn.sigmoid(gate_pre)
        active = gate_pre * sigmoid_gate
        hidden = (active * up_pre).astype(jnp.bfloat16)
        expert_out = jnp.dot(hidden, down_matrix.T, preferred_element_type=jnp.float32).astype(jnp.bfloat16)
        down_back = jnp.dot(flat_grad, down_matrix, preferred_element_type=jnp.float32)
        silu_slope = sigmoid_gate * (1.0 + gate_pre * (1.0 - sigmoid_gate))
        grad_gate_pre = (down_back * up_pre * silu_slope).astype(jnp.bfloat16)
        grad_up_pre = (down_back * active).astype(jnp.bfloat16)
        input_back = (jnp.dot(grad_gate_pre, gate_matrix.T, preferred_element_type=jnp.float32)
                      + jnp.dot(grad_up_pre, up_matrix.T, preferred_element_type=jnp.float32)).astype(jnp.bfloat16)
        flat_token = token_safe.reshape(-1)
        flat_pair = pair_safe.reshape(-1)
        out_float = expert_out.astype(jnp.float32)
        out_sum = out_sum.at[flat_block, flat_token].add(gate_value[:, None] * out_float)
        back_sum = back_sum.at[flat_block, flat_token].add(input_back.astype(jnp.float32) * live_float[:, None])
        product = jnp.sum(out_float * flat_grad_raw.astype(jnp.float32), axis=1) * live_float
        gate_grad = gate_grad.at[flat_block, flat_pair].add(product)
        grad_gate_w = group_gradient(flat_in, grad_gate_pre, group_count)
        grad_up_w = group_gradient(flat_in, grad_up_pre, group_count)
        grad_down_w = group_gradient(flat_grad, hidden, group_count)
        return (out_sum, back_sum, gate_grad), (grad_gate_w, grad_up_w, grad_down_w)

    initial = (jnp.zeros((block_count, TOK_DEV, D), jnp.float32),
               jnp.zeros((block_count, TOK_DEV, D), jnp.float32),
               jnp.zeros((block_count, pair_count), jnp.float32))
    totals, grads = lax.scan(per_expert, initial, jnp.arange(EXPERTS, dtype=jnp.int32))
    layer_out = totals[0].reshape(TOKENS, D).astype(jnp.bfloat16)
    grad_tokens = totals[1].reshape(TOKENS, D).astype(jnp.bfloat16)
    grad_gates = totals[2].reshape(TOKENS, TOPK)
    return layer_out, grad_tokens, grad_gates, grads[0], grads[1], grads[2]
```

```python
import functools

import jax
import jax.numpy as jnp
from jax import lax
from jax.experimental import pallas as pl
from jax.experimental.pallas import tpu as pltpu
from jax.sharding import PartitionSpec as P

UNITS = (2, 2, 2)
BF16 = jnp.bfloat16
F32 = jnp.float32
VMEM_LIMIT = 56 * 2**20
WHOLE = pl.BlockSpec(memory_space=pltpu.VMEM)
SCALAR = pl.BlockSpec(memory_space=pltpu.SMEM)


def dot(a, b, ca, cb):
    return lax.dot_general(a, b, (((ca,), (cb,)), ((), ())), preferred_element_type=F32)


def call(body, name, out_shape, in_specs, flops, moved, **extra):
    return pl.pallas_call(
        body,
        name=name,
        out_shape=out_shape,
        in_specs=in_specs,
        compiler_params=pltpu.CompilerParams(vmem_limit_bytes=VMEM_LIMIT),
        cost_estimate=pl.CostEstimate(flops=flops, bytes_accessed=moved, transcendentals=0),
        **extra,
    )


def after(x, *done):
    return lax.optimization_barrier((x, *done))[0] if done else x


def dispatch_body(n, index_ref, target_ref, gates_ref, tokens_ref, grad_ref, out_ref):
    experts, cap = out_ref.shape[0], out_ref.shape[1] // 2
    top_k, tok_dev = target_ref.shape
    feat = tokens_ref.shape[1] // n
    slots = experts * cap
    slot = lax.broadcasted_iota(jnp.int32, (slots, tok_dev), 0)
    pick = jnp.zeros((slots, tok_dev), F32)
    gate = jnp.zeros((slots, 1), F32)
    for k in range(top_k):
        hit = slot == target_ref[k : k + 1, :]
        pick = pick + jnp.where(hit, 1.0, 0.0)
        gate = gate + jnp.sum(jnp.where(hit, gates_ref[k : k + 1, :], 0.0), axis=1, keepdims=True)
    pick = pick.astype(BF16)
    for m in range(n):
        here = slice(m * feat, (m + 1) * feat)
        from_ = pl.ds(pl.multiple_of(lax.rem(index_ref[0] + m, n) * feat, 128), feat)
        rows = dot(pick, tokens_ref[:, from_], 1, 0).astype(BF16)
        grows = (dot(pick, grad_ref[:, from_], 1, 0) * gate).astype(BF16)
        out_ref[:, :cap, here] = rows.reshape(experts, cap, feat)
        out_ref[:, cap:, here] = grows.reshape(experts, cap, feat)


def dispatch(index, target, gates, tokens, grad_out, experts, cap, n):
    width = tokens.shape[1]
    return call(
        functools.partial(dispatch_body, n),
        "dispatch",
        jax.ShapeDtypeStruct((experts, 2 * cap, width), BF16),
        [SCALAR, WHOLE, WHOLE, WHOLE, WHOLE],
        4 * experts * cap * tokens.shape[0] * width,
        4 * (experts * cap + tokens.shape[0]) * width,
        out_specs=WHOLE,
    )(index, target, gates, tokens, grad_out)


def part_body(n, index_ref, rows_ref, *refs):
    own, above, below = refs[0], refs[1:n], refs[n : 2 * n - 1]
    full_ref, hid_ref, both_ref = refs[2 * n - 1 : 2 * n + 2]
    terms = refs[2 * n + 2 :]
    feat, three = own.shape
    f = three // 3
    experts, cap = rows_ref.shape[0], rows_ref.shape[1] // 2
    slots = experts * cap
    full_ref[:feat] = own[...]
    for m in range(1, n):
        inside = index_ref[0] + m < n

        @pl.when(inside)
        def _():
            full_ref[m * feat : (m + 1) * feat] = above[m - 1][...]

        @pl.when(jnp.logical_not(inside))
        def _():
            full_ref[m * feat : (m + 1) * feat] = below[n - m - 1][...]

    group = max(1, 128 // cap)
    tile = group * cap

    def forward(t, carry):
        at = pl.ds(pl.multiple_of(t * tile, tile), tile)
        of = pl.ds(t * group, group)
        pre = dot(rows_ref[of, :cap, :].reshape(tile, -1), full_ref[:, : 2 * f], 1, 0)
        gate_pre, up_pre = pre[:, :f], pre[:, f:]
        down_back = dot(rows_ref[of, cap:, :].reshape(tile, -1), full_ref[:, 2 * f :], 1, 0)
        sig = jax.nn.sigmoid(gate_pre)
        active = gate_pre * sig
        hid_ref[at, :] = (active * up_pre).astype(BF16)
        slope = sig * (1.0 + gate_pre * (1.0 - sig))
        both_ref[at, :f] = (down_back * up_pre * slope).astype(BF16)
        both_ref[at, f:] = (down_back * active).astype(BF16)
        return carry

    lax.fori_loop(0, slots // tile, forward, 0)
    for m in range(n):
        cols = slice(m * feat, (m + 1) * feat)
        rows = rows_ref[:, :cap, cols].reshape(slots, feat)
        grows = rows_ref[:, cap:, cols].reshape(slots, feat)
        terms[m][:, : 2 * f] = dot(rows, both_ref[...], 0, 0).astype(BF16)
        terms[m][:, 2 * f :] = dot(grows, hid_ref[...], 0, 0).astype(BF16)


def part(index, rows, own, above, below, n):
    feat, three = own.shape
    experts, double, width = rows.shape
    slots = experts * double // 2
    f = three // 3
    sds = jax.ShapeDtypeStruct
    out_shape = [sds((width, three), BF16), sds((slots, f), BF16), sds((slots, 2 * f), BF16)]
    out_shape += [sds((feat, three), BF16)] * n
    res = call(
        functools.partial(part_body, n),
        "part",
        out_shape,
        [SCALAR] + [WHOLE] * (2 * n),
        12 * slots * width * f,
        2 * (2 * slots * width + 3 * width * three),
        out_specs=[WHOLE] * len(out_shape),
    )(index, rows, own, *above, *below)
    return res[0], res[1], res[2], list(res[3:])


def back_body(count, cap, *refs):
    hids, boths, fulls = refs[:count], refs[count : 2 * count], refs[2 * count : 3 * count]
    out_ref = refs[3 * count]
    experts, _, feat = out_ref.shape
    out = back = None
    for hid, both, full in zip(hids, boths, fulls):
        f = hid.shape[1]
        o = dot(hid[...], full[:, 2 * f :], 1, 1)
        b = dot(both[...], full[:, : 2 * f], 1, 1)
        out, back = (o, b) if out is None else (out + o, back + b)
    out_ref[:, :cap, :] = out.astype(BF16).reshape(experts, cap, feat)
    out_ref[:, cap:, :] = back.astype(BF16).reshape(experts, cap, feat)


def back_products(hids, boths, fulls, experts, n):
    count = len(hids)
    slots = hids[0].shape[0]
    cap = slots // experts
    width = fulls[0].shape[0]
    feat = width // n
    ffn = sum(h.shape[1] for h in hids)
    return pl.pallas_call(
        functools.partial(back_body, count, cap),
        name="back_products",
        out_shape=jax.ShapeDtypeStruct((experts, 2 * cap, width), BF16),
        grid=(n,),
        in_specs=[pl.BlockSpec(x.shape, lambda m: (0, 0)) for x in (*hids, *boths)]
        + [pl.BlockSpec((feat, x.shape[1]), lambda m: (m, 0)) for x in fulls],
        out_specs=pl.BlockSpec((experts, 2 * cap, feat), lambda m: (0, 0, m)),
        compiler_params=pltpu.CompilerParams(vmem_limit_bytes=VMEM_LIMIT),
        cost_estimate=pl.CostEstimate(
            flops=6 * slots * width * ffn,
            bytes_accessed=2 * (3 * ffn * width + 2 * slots * width),
            transcendentals=0,
        ),
    )(*hids, *boths, *fulls)


def combine_body(n, index_ref, target_ref, gates_ref, grad_ref, rows_ref, out_ref, dtok_ref, dgate_ref):
    tok_dev, top_k = target_ref.shape
    experts, cap = rows_ref.shape[0], rows_ref.shape[1] // 2
    slots = experts * cap
    feat = rows_ref.shape[2] // n
    slot = lax.broadcasted_iota(jnp.int32, (tok_dev, slots), 1)
    hits = [jnp.where(slot == target_ref[:, k : k + 1], 1.0, 0.0) for k in range(top_k)]
    either = sum(hits).astype(BF16)
    hits = [h.astype(BF16) for h in hits]
    sums = [jnp.zeros((tok_dev, 1), F32) for _ in range(top_k)]
    for m in range(n):
        here = slice(m * feat, (m + 1) * feat)
        to = pl.ds(pl.multiple_of(lax.rem(index_ref[0] + m, n) * feat, 128), feat)
        total = jnp.zeros((tok_dev, feat), F32)
        grad = grad_ref[:, to].astype(F32)
        rows = rows_ref[:, :cap, here].reshape(slots, feat)
        for k in range(top_k):
            picked = dot(hits[k], rows, 1, 0)
            total = total + picked * gates_ref[:, k : k + 1]
            sums[k] = sums[k] + jnp.sum(picked * grad, axis=1, keepdims=True)
        out_ref[:, to] = total.astype(BF16)
        dtok_ref[:, to] = dot(either, rows_ref[:, cap:, here].reshape(slots, feat), 1, 0).astype(BF16)
    for k in range(top_k):
        dgate_ref[:, k : k + 1] = sums[k]


def combine(index, target, gates, grad_out, rows, n):
    shape = jax.ShapeDtypeStruct(grad_out.shape, BF16)
    return call(
        functools.partial(combine_body, n),
        "combine",
        [shape, shape, jax.ShapeDtypeStruct(gates.shape, F32)],
        [SCALAR, WHOLE, WHOLE, WHOLE, WHOLE],
        3 * rows.shape[0] * rows.shape[1] * grad_out.size,
        2 * (rows.size + 3 * grad_out.size),
        out_specs=[WHOLE, WHOLE, WHOLE],
    )(index, target, gates, grad_out, rows)


def gather_step(step, n, up, down):
    return (
        lax.ppermute(up, "dp", [(j, j + 1) for j in range(step - 1, n - 1)]),
        lax.ppermute(down, "dp", [(j, j - 1) for j in range(n - step, 0, -1)]),
    )


def scatter_step(step, n, up, down):
    return (
        lax.ppermute(up, "dp", [(j, j + 1) for j in range(step)]),
        lax.ppermute(down, "dp", [(j, j - 1) for j in range(n - 1, n - 1 - step, -1)]),
    )


def add(a, b):
    return (a.astype(F32) + b.astype(F32)).astype(BF16)


def exchange(rows):
    return lax.all_to_all(rows, "expert", split_axis=0, concat_axis=0, tiled=True)


class Gather:
    def __init__(self, own, n):
        self.own, self.n, self.step = own, n, 0
        self.last = (own, own)
        self.below, self.above = [], []

    def go(self, waits=()):
        self.step += 1
        up, down = (after(x, *waits) for x in self.last)
        self.last = gather_step(self.step, self.n, up, down)
        self.below.append(self.last[0])
        self.above.append(self.last[1])


class Scatter:
    def __init__(self, terms, n):
        self.terms, self.n, self.step = terms, n, 0
        self.last = ()

    def go(self, waits=()):
        terms, n, step = self.terms, self.n, self.step
        if step:
            up, down = add(self.last[0], terms[n - 1 - step]), add(self.last[1], terms[step + 1])
        else:
            up, down = terms[n - 1], terms[1]
        self.step += 1
        self.last = scatter_step(self.step, n, after(up, *waits), after(down, *waits))

    def result(self):
        up, down = self.last
        return (up.astype(F32) + down.astype(F32) + self.terms[0].astype(F32)).astype(BF16)


def on_device(tokens, expert_ids, slot_index, routing_gates, grad_out, w_gate, w_up, w_down):
    tok_dev, top_k = expert_ids.shape
    experts = lax.axis_size("expert")
    n = lax.axis_size("dp")
    index = lax.axis_index("dp").astype(jnp.int32).reshape(1)
    capacity = 2 * tok_dev * top_k // experts
    unit = w_gate.shape[2] // sum(UNITS)
    edges = [sum(UNITS[:c]) * unit for c in range(len(UNITS) + 1)]
    spans = [slice(a, b) for a, b in zip(edges, edges[1:])]
    count = len(spans)

    owns = [jnp.concatenate([w[0, :, s] for w in (w_gate, w_up, w_down)], axis=1) for s in spans]
    target = expert_ids * capacity + slot_index
    if DISPATCH_AFTER_PACK:
        target = after(target, owns[0])
    sent = dispatch(index, target.T, routing_gates.T, tokens, grad_out, experts, capacity, n)

    fulls, hids, boths = [], [], []
    gathers = [Gather(own, n) for own in owns]
    scatters = []

    def run_part(c, waits=()):
        g = gathers[c]
        full, hid, both, terms = part(index, after(rows, *waits), g.own, g.above, g.below, n)
        fulls.append(full)
        hids.append(hid)
        boths.append(both)
        scatters.append(Scatter(terms, n))

    gathers[0].go()
    if EXCHANGE_AFTER_GATHER:
        sent = after(sent, *gathers[0].last)
    rows = exchange(sent)
    for _ in range(n - 2):
        gathers[0].go()
    history = [gathers[0].last]
    for c in range(1, count):
        for step in range(1, n):
            if step == 2:
                run_part(c - 1, PART_WAITS and sum(history[-1:], ()))
            waits = sum(history[-LAG:-LAG + 1 or None], ())
            if step == 2 and GATHER_AFTER_PART:
                waits += (hids[-1],)
            gathers[c].go(waits)
            done = gathers[c].last
            for s in scatters:
                if s.step < n - 1:
                    s.go()
                    done += s.last
            history.append(done)
    run_part(count - 1, TAIL_WAITS and sum(history[-1:], ()))
    old = scatters[-2] if count > 1 else None
    if old is not None:
        while old.step < n - 1:
            old.go()
    if SERIAL_TAIL:
        scatters[-1].go(old.last)
    out = back_products(hids, boths, fulls, experts, n)
    if RETURN_AFTER_SCATTER:
        if not SERIAL_TAIL:
            scatters[-1].go()
        out = after(out, *scatters[-1].last)
    returned = exchange(out)
    for s in scatters:
        while s.step < n - 1:
            s.go()
    grads = [s.result() for s in scatters]

    layer_out, grad_tokens, grad_gates = combine(index, target, routing_gates, grad_out, returned, n)
    stacked = []
    for k in range(3):
        pieces = []
        for s, g in zip(spans, grads):
            f = s.stop - s.start
            pieces.append(g[:, k * f : (k + 1) * f])
        stacked.append(jnp.concatenate(pieces, axis=1)[None])
    return (layer_out, grad_tokens, grad_gates, *stacked)


DISPATCH_AFTER_PACK = True
EXCHANGE_AFTER_GATHER = True
GATHER_AFTER_PART = True
PART_WAITS = ()
TAIL_WAITS = True
SERIAL_TAIL = False
RETURN_AFTER_SCATTER = False
LAG = 1


def solution(mesh):
    in_specs = (P(("dp", "expert"), None),) * 5 + (P("expert", "dp", None),) * 3
    out_specs = (P(("dp", "expert"), None),) * 3 + (P("expert", "dp", None),) * 3
    return jax.shard_map(
        on_device, mesh=mesh, in_specs=in_specs, out_specs=out_specs, check_vma=False
    )
```

```python
import functools

import jax
import jax.numpy as jnp
from jax import lax
from jax.experimental import pallas as pl
from jax.experimental.pallas import tpu as pltpu
from jax.sharding import PartitionSpec as P

UNITS = (2, 2, 2)
BF16 = jnp.bfloat16
F32 = jnp.float32
VMEM_LIMIT = 18 * 2**20
WHOLE = pl.BlockSpec(memory_space=pltpu.VMEM)
SCALAR = pl.BlockSpec(memory_space=pltpu.SMEM)


def dot(a, b, ca, cb):
    return lax.dot_general(a, b, (((ca,), (cb,)), ((), ())), preferred_element_type=F32)


def call(body, name, out_shape, in_specs, flops, moved, **extra):
    return pl.pallas_call(
        body,
        name=name,
        out_shape=out_shape,
        in_specs=in_specs,
        compiler_params=pltpu.CompilerParams(vmem_limit_bytes=VMEM_LIMIT),
        cost_estimate=pl.CostEstimate(flops=flops, bytes_accessed=moved, transcendentals=0),
        **extra,
    )


def after(x, *done):
    return lax.optimization_barrier((x, *done))[0] if done else x


def dispatch_body(n, index_ref, target_ref, gates_ref, tokens_ref, grad_ref, out_ref):
    experts, cap = out_ref.shape[0], out_ref.shape[1] // 2
    top_k, tok_dev = target_ref.shape
    feat = tokens_ref.shape[1] // n
    slots = experts * cap
    slot = lax.broadcasted_iota(jnp.int32, (slots, tok_dev), 0)
    pick = jnp.zeros((slots, tok_dev), F32)
    gate = jnp.zeros((slots, 1), F32)
    for k in range(top_k):
        hit = slot == target_ref[k : k + 1, :]
        pick = pick + jnp.where(hit, 1.0, 0.0)
        gate = gate + jnp.sum(jnp.where(hit, gates_ref[k : k + 1, :], 0.0), axis=1, keepdims=True)
    pick = pick.astype(BF16)
    for m in range(n):
        here = slice(m * feat, (m + 1) * feat)
        from_ = pl.ds(pl.multiple_of(lax.rem(index_ref[0] + m, n) * feat, 128), feat)
        rows = dot(pick, tokens_ref[:, from_], 1, 0).astype(BF16)
        grows = (dot(pick, grad_ref[:, from_], 1, 0) * gate).astype(BF16)
        out_ref[:, :cap, here] = rows.reshape(experts, cap, feat)
        out_ref[:, cap:, here] = grows.reshape(experts, cap, feat)


def dispatch(index, target, gates, tokens, grad_out, experts, cap, n):
    width = tokens.shape[1]
    return call(
        functools.partial(dispatch_body, n),
        "dispatch",
        jax.ShapeDtypeStruct((experts, 2 * cap, width), BF16),
        [SCALAR, WHOLE, WHOLE, WHOLE, WHOLE],
        4 * experts * cap * tokens.shape[0] * width,
        4 * (experts * cap + tokens.shape[0]) * width,
        out_specs=WHOLE,
    )(index, target, gates, tokens, grad_out)


def part_body(n, split, index_ref, rows_ref, *refs):
    own, above, below = refs[0], refs[1:n], refs[n : 2 * n - 1]
    full_ref, hid_ref, both_ref = refs[2 * n - 1 : 2 * n + 2]
    terms = refs[2 * n + 2 :]
    feat, three = own.shape
    f = three // 3
    experts, cap = rows_ref.shape[0], rows_ref.shape[1] // 2
    slots = experts * cap
    full_ref[:feat] = own[...]
    for m in range(1, n):
        inside = index_ref[0] + m < n

        @pl.when(inside)
        def _():
            full_ref[m * feat : (m + 1) * feat] = above[m - 1][...]

        @pl.when(jnp.logical_not(inside))
        def _():
            full_ref[m * feat : (m + 1) * feat] = below[n - m - 1][...]

    group = max(1, 128 // cap)
    tile = group * cap

    def forward(t, carry):
        at = pl.ds(pl.multiple_of(t * tile, tile), tile)
        of = pl.ds(t * group, group)
        pre = dot(rows_ref[of, :cap, :].reshape(tile, -1), full_ref[:, : 2 * f], 1, 0)
        gate_pre, up_pre = pre[:, :f], pre[:, f:]
        down_back = dot(rows_ref[of, cap:, :].reshape(tile, -1), full_ref[:, 2 * f :], 1, 0)
        sig = jax.nn.sigmoid(gate_pre)
        active = gate_pre * sig
        hid_ref[at, :] = (active * up_pre).astype(BF16)
        slope = sig * (1.0 + gate_pre * (1.0 - sig))
        both_ref[at, :f] = (down_back * up_pre * slope).astype(BF16)
        both_ref[at, f:] = (down_back * active).astype(BF16)
        return carry

    lax.fori_loop(0, slots // tile, forward, 0)
    for m in range(n):
        cols = slice(m * feat, (m + 1) * feat)
        rows = rows_ref[:, :cap, cols].reshape(slots, feat)
        grows = rows_ref[:, cap:, cols].reshape(slots, feat)
        inner = dot(rows, both_ref[...], 0, 0).astype(BF16)
        outer = dot(grows, hid_ref[...], 0, 0).astype(BF16)
        if split:
            terms[m][...] = inner
            terms[n + m][...] = outer
        else:
            terms[m][:, : 2 * f] = inner
            terms[m][:, 2 * f :] = outer


def part(index, rows, own, above, below, n, split=False):
    feat, three = own.shape
    experts, double, width = rows.shape
    slots = experts * double // 2
    f = three // 3
    sds = jax.ShapeDtypeStruct
    out_shape = [sds((width, three), BF16), sds((slots, f), BF16), sds((slots, 2 * f), BF16)]
    for columns in (2 * f, f) if split else (three,):
        out_shape += [sds((feat, columns), BF16)] * n
    res = call(
        functools.partial(part_body, n, split),
        "part",
        out_shape,
        [SCALAR] + [WHOLE] * (2 * n),
        12 * slots * width * f,
        2 * (2 * slots * width + 3 * width * three),
        out_specs=[WHOLE] * len(out_shape),
    )(index, rows, own, *above, *below)
    return res[0], res[1], res[2], list(res[3:])


def back_body(count, cap, *refs):
    hids, boths, fulls = refs[:count], refs[count : 2 * count], refs[2 * count : 3 * count]
    out_ref = refs[3 * count]
    experts, _, feat = out_ref.shape
    out = back = None
    for hid, both, full in zip(hids, boths, fulls):
        f = hid.shape[1]
        o = dot(hid[...], full[:, 2 * f :], 1, 1)
        b = dot(both[...], full[:, : 2 * f], 1, 1)
        out, back = (o, b) if out is None else (out + o, back + b)
    out_ref[:, :cap, :] = out.astype(BF16).reshape(experts, cap, feat)
    out_ref[:, cap:, :] = back.astype(BF16).reshape(experts, cap, feat)


def back_products(hids, boths, fulls, experts, n):
    count = len(hids)
    slots = hids[0].shape[0]
    cap = slots // experts
    width = fulls[0].shape[0]
    feat = width // n
    ffn = sum(h.shape[1] for h in hids)
    return pl.pallas_call(
        functools.partial(back_body, count, cap),
        name="back_products",
        out_shape=jax.ShapeDtypeStruct((experts, 2 * cap, width), BF16),
        grid=(n,),
        in_specs=[pl.BlockSpec(x.shape, lambda m: (0, 0)) for x in (*hids, *boths)]
        + [pl.BlockSpec((feat, x.shape[1]), lambda m: (m, 0)) for x in fulls],
        out_specs=pl.BlockSpec((experts, 2 * cap, feat), lambda m: (0, 0, m)),
        compiler_params=pltpu.CompilerParams(vmem_limit_bytes=VMEM_LIMIT),
        cost_estimate=pl.CostEstimate(
            flops=6 * slots * width * ffn,
            bytes_accessed=2 * (3 * ffn * width + 2 * slots * width),
            transcendentals=0,
        ),
    )(*hids, *boths, *fulls)


def combine_body(n, index_ref, target_ref, gates_ref, grad_ref, rows_ref, out_ref, dtok_ref, dgate_ref):
    tok_dev, top_k = target_ref.shape
    experts, cap = rows_ref.shape[0], rows_ref.shape[1] // 2
    slots = experts * cap
    feat = rows_ref.shape[2] // n
    slot = lax.broadcasted_iota(jnp.int32, (tok_dev, slots), 1)
    hits = [jnp.where(slot == target_ref[:, k : k + 1], 1.0, 0.0) for k in range(top_k)]
    either = sum(hits).astype(BF16)
    hits = [h.astype(BF16) for h in hits]
    sums = [jnp.zeros((tok_dev, 1), F32) for _ in range(top_k)]
    for m in range(n):
        here = slice(m * feat, (m + 1) * feat)
        to = pl.ds(pl.multiple_of(lax.rem(index_ref[0] + m, n) * feat, 128), feat)
        total = jnp.zeros((tok_dev, feat), F32)
        grad = grad_ref[:, to].astype(F32)
        rows = rows_ref[:, :cap, here].reshape(slots, feat)
        for k in range(top_k):
            picked = dot(hits[k], rows, 1, 0)
            total = total + picked * gates_ref[:, k : k + 1]
            sums[k] = sums[k] + jnp.sum(picked * grad, axis=1, keepdims=True)
        out_ref[:, to] = total.astype(BF16)
        dtok_ref[:, to] = dot(either, rows_ref[:, cap:, here].reshape(slots, feat), 1, 0).astype(BF16)
    for k in range(top_k):
        dgate_ref[:, k : k + 1] = sums[k]


def combine(index, target, gates, grad_out, rows, n):
    shape = jax.ShapeDtypeStruct(grad_out.shape, BF16)
    return call(
        functools.partial(combine_body, n),
        "combine",
        [shape, shape, jax.ShapeDtypeStruct(gates.shape, F32)],
        [SCALAR, WHOLE, WHOLE, WHOLE, WHOLE],
        3 * rows.shape[0] * rows.shape[1] * grad_out.size,
        2 * (rows.size + 3 * grad_out.size),
        out_specs=[WHOLE, WHOLE, WHOLE],
    )(index, target, gates, grad_out, rows)


def gather_step(step, n, up, down):
    return (
        lax.ppermute(up, "dp", [(j, j + 1) for j in range(step - 1, n - 1)]),
        lax.ppermute(down, "dp", [(j, j - 1) for j in range(n - step, 0, -1)]),
    )


def scatter_step(step, n, up, down):
    return (
        lax.ppermute(up, "dp", [(j, j + 1) for j in range(step)]),
        lax.ppermute(down, "dp", [(j, j - 1) for j in range(n - 1, n - 1 - step, -1)]),
    )


def add(a, b):
    return (a.astype(F32) + b.astype(F32)).astype(BF16)


def exchange(rows):
    return lax.all_to_all(rows, "expert", split_axis=0, concat_axis=0, tiled=True)


class Gather:
    def __init__(self, own, n):
        self.own, self.n, self.step = own, n, 0
        self.last = (own, own)
        self.below, self.above = [], []

    def go(self, waits=()):
        self.step += 1
        up, down = (after(x, *waits) for x in self.last)
        self.last = gather_step(self.step, self.n, up, down)
        self.below.append(self.last[0])
        self.above.append(self.last[1])


class Scatter:
    def __init__(self, terms, n):
        self.terms, self.n, self.step = terms, n, 0
        self.last = ()

    def go(self, waits=()):
        terms, n, step = self.terms, self.n, self.step
        if step:
            up, down = add(self.last[0], terms[n - 1 - step]), add(self.last[1], terms[step + 1])
        else:
            up, down = terms[n - 1], terms[1]
        self.step += 1
        self.last = scatter_step(self.step, n, after(up, *waits), after(down, *waits))

    def result(self):
        up, down = self.last
        return (up.astype(F32) + down.astype(F32) + self.terms[0].astype(F32)).astype(BF16)


def on_device(tokens, expert_ids, slot_index, routing_gates, grad_out, w_gate, w_up, w_down):
    tok_dev, top_k = expert_ids.shape
    experts = lax.axis_size("expert")
    n = lax.axis_size("dp")
    index = lax.axis_index("dp").astype(jnp.int32).reshape(1)
    capacity = 2 * tok_dev * top_k // experts
    unit = w_gate.shape[2] // sum(UNITS)
    edges = [sum(UNITS[:c]) * unit for c in range(len(UNITS) + 1)]
    spans = [slice(a, b) for a, b in zip(edges, edges[1:])]
    count = len(spans)

    owns = [jnp.concatenate([w[0, :, s] for w in (w_gate, w_up, w_down)], axis=1) for s in spans]
    target = expert_ids * capacity + slot_index
    if DISPATCH_AFTER_PACK:
        target = after(target, owns[0])
    sent = dispatch(index, target.T, routing_gates.T, tokens, grad_out, experts, capacity, n)

    fulls, hids, boths = [], [], []
    gathers = [Gather(own, n) for own in owns]
    scatters = []

    def run_part(c, waits=()):
        g = gathers[c]
        split = SPLIT_LAST and c == count - 1
        full, hid, both, terms = part(index, after(rows, *waits), g.own, g.above, g.below, n, split)
        fulls.append(full)
        hids.append(hid)
        boths.append(both)
        scatters.append([Scatter(terms[k * n : (k + 1) * n], n) for k in range(1 + split)])

    gathers[0].go()
    if EXCHANGE_AFTER_GATHER:
        sent = after(sent, *gathers[0].last)
    rows = exchange(sent)
    for _ in range(n - 2):
        gathers[0].go()
    history = [gathers[0].last]
    for c in range(1, count):
        for step in range(1, n):
            if step == 2:
                run_part(c - 1)
            waits = sum(history[-LAG:-LAG + 1 or None], ())
            if step == 1 and c == 1 and EARLY:
                waits = (gathers[0].below[-2], gathers[0].above[-2])
            if step == 2 and GATHER_AFTER_PART:
                waits += (hids[-1],)
            gathers[c].go(waits)
            done = gathers[c].last
            for (s,) in scatters:
                if s.step < n - 1:
                    s.go()
                    done += s.last
            history.append(done)
    run_part(count - 1, TAIL_WAITS and sum(history[-1:], ()))
    old = scatters[-2][0]
    while old.step < n - 1:
        old.go()
    if SERIAL_TAIL:
        scatters[-1][0].go(old.last)
    out = back_products(hids, boths, fulls, experts, n)
    if RETURN_AFTER == 1:
        out = after(out, *old.last)
    if RETURN_AFTER == 2:
        scatters[-1][0].go()
        out = after(out, *scatters[-1][0].last)
    returned = exchange(out)
    for _ in range(n - 1):
        for s in scatters[-1]:
            if s.step < n - 1:
                s.go()
    layer_out, grad_tokens, grad_gates = combine(index, target, routing_gates, grad_out, returned, n)
    if COMBINE_EARLY:
        for s in scatters[-1]:
            s.last = tuple(after(x, layer_out) for x in s.last)
    grads = [[s.result() for s in group] for group in scatters]
    stacked = []
    for k in range(3):
        pieces = []
        for s, g in zip(spans, grads):
            f = s.stop - s.start
            pieces.append(
                g[k // 2][:, (k % 2) * f : (k % 2 + 1) * f] if len(g) == 2 else g[0][:, k * f : (k + 1) * f]
            )
        stacked.append(jnp.concatenate(pieces, axis=1)[None])
    return (layer_out, grad_tokens, grad_gates, *stacked)


EARLY = False
SPLIT_LAST = False
COMBINE_EARLY = False
RETURN_AFTER = 1
DISPATCH_AFTER_PACK = True
EXCHANGE_AFTER_GATHER = True
GATHER_AFTER_PART = True
TAIL_WAITS = True
SERIAL_TAIL = False
LAG = 1


def solution(mesh):
    in_specs = (P(("dp", "expert"), None),) * 5 + (P("expert", "dp", None),) * 3
    out_specs = (P(("dp", "expert"), None),) * 3 + (P("expert", "dp", None),) * 3
    return jax.shard_map(
        on_device, mesh=mesh, in_specs=in_specs, out_specs=out_specs, check_vma=False
    )
```

```python
import functools

import jax
import jax.numpy as jnp
from jax import lax
from jax.experimental import pallas as pl
from jax.experimental.pallas import tpu as pltpu
from jax.sharding import PartitionSpec as P

UNITS = (2, 2, 2)
BF16 = jnp.bfloat16
F32 = jnp.float32
VMEM_LIMIT = 18 * 2**20
WHOLE = pl.BlockSpec(memory_space=pltpu.VMEM)
SCALAR = pl.BlockSpec(memory_space=pltpu.SMEM)


def dot(a, b, ca, cb):
    return lax.dot_general(a, b, (((ca,), (cb,)), ((), ())), preferred_element_type=F32)


def call(body, name, out_shape, in_specs, flops, moved, **extra):
    return pl.pallas_call(
        body,
        name=name,
        out_shape=out_shape,
        in_specs=in_specs,
        compiler_params=pltpu.CompilerParams(vmem_limit_bytes=VMEM_LIMIT),
        cost_estimate=pl.CostEstimate(flops=flops, bytes_accessed=moved, transcendentals=0),
        **extra,
    )


def after(x, *done):
    return lax.optimization_barrier((x, *done))[0] if done else x


def dispatch_body(n, index_ref, target_ref, gates_ref, tokens_ref, grad_ref, out_ref):
    experts, cap = out_ref.shape[0], out_ref.shape[1] // 2
    top_k, tok_dev = target_ref.shape
    feat = tokens_ref.shape[1] // n
    slots = experts * cap
    slot = lax.broadcasted_iota(jnp.int32, (slots, tok_dev), 0)
    pick = jnp.zeros((slots, tok_dev), F32)
    gate = jnp.zeros((slots, 1), F32)
    for k in range(top_k):
        hit = slot == target_ref[k : k + 1, :]
        pick = pick + jnp.where(hit, 1.0, 0.0)
        gate = gate + jnp.sum(jnp.where(hit, gates_ref[k : k + 1, :], 0.0), axis=1, keepdims=True)
    pick = pick.astype(BF16)
    for m in range(n):
        here = slice(m * feat, (m + 1) * feat)
        from_ = pl.ds(pl.multiple_of(lax.rem(index_ref[0] + m, n) * feat, 128), feat)
        rows = dot(pick, tokens_ref[:, from_], 1, 0).astype(BF16)
        grows = (dot(pick, grad_ref[:, from_], 1, 0) * gate).astype(BF16)
        out_ref[:, :cap, here] = rows.reshape(experts, cap, feat)
        out_ref[:, cap:, here] = grows.reshape(experts, cap, feat)


def dispatch(index, target, gates, tokens, grad_out, experts, cap, n):
    width = tokens.shape[1]
    return call(
        functools.partial(dispatch_body, n),
        "dispatch",
        jax.ShapeDtypeStruct((experts, 2 * cap, width), BF16),
        [SCALAR, WHOLE, WHOLE, WHOLE, WHOLE],
        4 * experts * cap * tokens.shape[0] * width,
        4 * (experts * cap + tokens.shape[0]) * width,
        out_specs=WHOLE,
    )(index, target, gates, tokens, grad_out)


def part_body(n, index_ref, rows_ref, *refs):
    own, above, below = refs[0], refs[1:n], refs[n : 2 * n - 1]
    full_ref, hid_ref, both_ref = refs[2 * n - 1 : 2 * n + 2]
    terms, sems = refs[2 * n + 2 : -1], refs[-1]
    feat, three = own.shape
    f = three // 3
    experts, cap = rows_ref.shape[0], rows_ref.shape[1] // 2
    slots = experts * cap

    def fetch(shard, m):
        return pltpu.make_async_copy(shard, full_ref.at[m * feat : (m + 1) * feat], sems.at[m])

    fetch(own, 0).start()
    for m in range(1, n):
        inside = index_ref[0] + m < n

        @pl.when(inside)
        def _():
            fetch(above[m - 1], m).start()

        @pl.when(jnp.logical_not(inside))
        def _():
            fetch(below[n - m - 1], m).start()

    for m in range(n):
        fetch(own, m).wait()
    group = max(1, 128 // cap)
    tile = group * cap

    def forward(t, carry):
        at = pl.ds(pl.multiple_of(t * tile, tile), tile)
        of = pl.ds(t * group, group)
        pre = dot(rows_ref[of, :cap, :].reshape(tile, -1), full_ref[:, : 2 * f], 1, 0)
        gate_pre, up_pre = pre[:, :f], pre[:, f:]
        down_back = dot(rows_ref[of, cap:, :].reshape(tile, -1), full_ref[:, 2 * f :], 1, 0)
        sig = jax.nn.sigmoid(gate_pre)
        active = gate_pre * sig
        hid_ref[at, :] = (active * up_pre).astype(BF16)
        slope = sig * (1.0 + gate_pre * (1.0 - sig))
        both_ref[at, :f] = (down_back * up_pre * slope).astype(BF16)
        both_ref[at, f:] = (down_back * active).astype(BF16)
        return carry

    lax.fori_loop(0, slots // tile, forward, 0)
    for m in range(n):
        cols = slice(m * feat, (m + 1) * feat)
        rows = rows_ref[:, :cap, cols].reshape(slots, feat)
        grows = rows_ref[:, cap:, cols].reshape(slots, feat)
        terms[m][:, : 2 * f] = dot(rows, both_ref[...], 0, 0).astype(BF16)
        terms[m][:, 2 * f :] = dot(grows, hid_ref[...], 0, 0).astype(BF16)


def part(index, rows, own, above, below, n):
    feat, three = own.shape
    experts, double, width = rows.shape
    slots = experts * double // 2
    f = three // 3
    sds = jax.ShapeDtypeStruct
    out_shape = [sds((width, three), BF16), sds((slots, f), BF16), sds((slots, 2 * f), BF16)]
    out_shape += [sds((feat, three), BF16)] * n
    res = call(
        functools.partial(part_body, n),
        "part",
        out_shape,
        [SCALAR, WHOLE] + [pl.BlockSpec(memory_space=pltpu.HBM)] * (2 * n - 1),
        12 * slots * width * f,
        2 * (2 * slots * width + 3 * width * three),
        out_specs=[WHOLE] * len(out_shape),
        scratch_shapes=[pltpu.SemaphoreType.DMA((n,))],
    )(index, rows, own, *above, *below)
    return res[0], res[1], res[2], list(res[3:])


def touch_body(index_ref, *refs):
    refs[-1][0] = index_ref[0]


def touch(index, arrays, weight):
    return call(
        touch_body,
        "touch",
        jax.ShapeDtypeStruct(index.shape, index.dtype),
        [SCALAR] + [pl.BlockSpec(memory_space=pl.ANY)] * len(arrays),
        weight,
        0,
        out_specs=SCALAR,
    )(index, *arrays)


def back_body(count, cap, *refs):
    hids, boths, fulls = refs[:count], refs[count : 2 * count], refs[2 * count : 3 * count]
    out_ref = refs[3 * count]
    experts, _, feat = out_ref.shape
    out = back = None
    for hid, both, full in zip(hids, boths, fulls):
        f = hid.shape[1]
        o = dot(hid[...], full[:, 2 * f :], 1, 1)
        b = dot(both[...], full[:, : 2 * f], 1, 1)
        out, back = (o, b) if out is None else (out + o, back + b)
    out_ref[:, :cap, :] = out.astype(BF16).reshape(experts, cap, feat)
    out_ref[:, cap:, :] = back.astype(BF16).reshape(experts, cap, feat)


def back_products(hids, boths, fulls, experts, n):
    count = len(hids)
    slots = hids[0].shape[0]
    cap = slots // experts
    width = fulls[0].shape[0]
    feat = width // n
    ffn = sum(h.shape[1] for h in hids)
    return pl.pallas_call(
        functools.partial(back_body, count, cap),
        name="back_products",
        out_shape=jax.ShapeDtypeStruct((experts, 2 * cap, width), BF16),
        grid=(n,),
        in_specs=[pl.BlockSpec(x.shape, lambda m: (0, 0)) for x in (*hids, *boths)]
        + [pl.BlockSpec((feat, x.shape[1]), lambda m: (m, 0)) for x in fulls],
        out_specs=pl.BlockSpec((experts, 2 * cap, feat), lambda m: (0, 0, m)),
        compiler_params=pltpu.CompilerParams(vmem_limit_bytes=VMEM_LIMIT),
        cost_estimate=pl.CostEstimate(
            flops=6 * slots * width * ffn,
            bytes_accessed=2 * (3 * ffn * width + 2 * slots * width),
            transcendentals=0,
        ),
    )(*hids, *boths, *fulls)


def combine_body(n, index_ref, target_ref, gates_ref, grad_ref, rows_ref, out_ref, dtok_ref, dgate_ref):
    tok_dev, top_k = target_ref.shape
    experts, cap = rows_ref.shape[0], rows_ref.shape[1] // 2
    slots = experts * cap
    feat = rows_ref.shape[2] // n
    slot = lax.broadcasted_iota(jnp.int32, (tok_dev, slots), 1)
    hits = [jnp.where(slot == target_ref[:, k : k + 1], 1.0, 0.0) for k in range(top_k)]
    either = sum(hits).astype(BF16)
    hits = [h.astype(BF16) for h in hits]
    sums = [jnp.zeros((tok_dev, 1), F32) for _ in range(top_k)]
    for m in range(n):
        here = slice(m * feat, (m + 1) * feat)
        to = pl.ds(pl.multiple_of(lax.rem(index_ref[0] + m, n) * feat, 128), feat)
        total = jnp.zeros((tok_dev, feat), F32)
        grad = grad_ref[:, to].astype(F32)
        rows = rows_ref[:, :cap, here].reshape(slots, feat)
        for k in range(top_k):
            picked = dot(hits[k], rows, 1, 0)
            total = total + picked * gates_ref[:, k : k + 1]
            sums[k] = sums[k] + jnp.sum(picked * grad, axis=1, keepdims=True)
        out_ref[:, to] = total.astype(BF16)
        dtok_ref[:, to] = dot(either, rows_ref[:, cap:, here].reshape(slots, feat), 1, 0).astype(BF16)
    for k in range(top_k):
        dgate_ref[:, k : k + 1] = sums[k]


def combine(index, target, gates, grad_out, rows, n):
    shape = jax.ShapeDtypeStruct(grad_out.shape, BF16)
    return call(
        functools.partial(combine_body, n),
        "combine",
        [shape, shape, jax.ShapeDtypeStruct(gates.shape, F32)],
        [SCALAR, WHOLE, WHOLE, WHOLE, WHOLE],
        3 * rows.shape[0] * rows.shape[1] * grad_out.size,
        2 * (rows.size + 3 * grad_out.size),
        out_specs=[WHOLE, WHOLE, WHOLE],
    )(index, target, gates, grad_out, rows)


def gather_step(step, n, up, down):
    return (
        lax.ppermute(up, "dp", [(j, j + 1) for j in range(step - 1, n - 1)]),
        lax.ppermute(down, "dp", [(j, j - 1) for j in range(n - step, 0, -1)]),
    )


def scatter_step(step, n, up, down):
    return (
        lax.ppermute(up, "dp", [(j, j + 1) for j in range(step)]),
        lax.ppermute(down, "dp", [(j, j - 1) for j in range(n - 1, n - 1 - step, -1)]),
    )


def add(a, b):
    return (a.astype(F32) + b.astype(F32)).astype(BF16)


def exchange(rows):
    return lax.all_to_all(rows, "expert", split_axis=0, concat_axis=0, tiled=True)


class Gather:
    def __init__(self, own, n):
        self.own, self.n, self.step = own, n, 0
        self.last = (own, own)
        self.below, self.above = [], []

    def go(self, waits=()):
        self.step += 1
        up, down = (after(x, *waits) for x in self.last)
        self.last = gather_step(self.step, self.n, up, down)
        self.below.append(self.last[0])
        self.above.append(self.last[1])


class Scatter:
    def __init__(self, terms, n):
        self.terms, self.n, self.step = terms, n, 0
        self.last = ()

    def go(self, waits=()):
        terms, n, step = self.terms, self.n, self.step
        if step:
            up, down = add(self.last[0], terms[n - 1 - step]), add(self.last[1], terms[step + 1])
        else:
            up, down = terms[n - 1], terms[1]
        self.step += 1
        self.last = scatter_step(self.step, n, after(up, *waits), after(down, *waits))

    def result(self):
        up, down = self.last
        return (up.astype(F32) + down.astype(F32) + self.terms[0].astype(F32)).astype(BF16)


def on_device(tokens, expert_ids, slot_index, routing_gates, grad_out, w_gate, w_up, w_down):
    tok_dev, top_k = expert_ids.shape
    experts = lax.axis_size("expert")
    n = lax.axis_size("dp")
    index = lax.axis_index("dp").astype(jnp.int32).reshape(1)
    capacity = 2 * tok_dev * top_k // experts
    unit = w_gate.shape[2] // sum(UNITS)
    edges = [sum(UNITS[:c]) * unit for c in range(len(UNITS) + 1)]
    spans = [slice(a, b) for a, b in zip(edges, edges[1:])]
    count = len(spans)

    owns = [jnp.concatenate([w[0, :, s] for w in (w_gate, w_up, w_down)], axis=1) for s in spans]
    target = expert_ids * capacity + slot_index
    if DISPATCH_AFTER_PACK:
        target = after(target, owns[0])
    sent = dispatch(index, target.T, routing_gates.T, tokens, grad_out, experts, capacity, n)

    fulls, hids, boths = [], [], []
    gathers = [Gather(own, n) for own in owns]
    scatters = []

    def run_part(c, waits=()):
        g = gathers[c]
        ready = touch(index, g.last, WEIGHT) if c == 0 else index
        full, hid, both, terms = part(ready, after(rows, *waits), g.own, g.above, g.below, n)
        fulls.append(full)
        hids.append(hid)
        boths.append(both)
        scatters.append([Scatter(terms, n)])

    gathers[0].go()
    if EXCHANGE_AFTER_GATHER:
        sent = after(sent, *gathers[0].last)
    rows = exchange(sent)
    for _ in range(n - 2):
        gathers[0].go()
    history = [gathers[0].last]
    for c in range(1, count):
        for step in range(1, n):
            if step == 2:
                run_part(c - 1)
            waits = sum(history[-LAG:-LAG + 1 or None], ())
            if step == 1 and c == 1 and EARLY:
                waits = (gathers[0].below[-2], gathers[0].above[-2])
            if step == 2 and GATHER_AFTER_PART:
                waits += (hids[-1],)
            gathers[c].go(waits)
            done = gathers[c].last
            for (s,) in scatters:
                if s.step < n - 1:
                    s.go()
                    done += s.last
            history.append(done)
    run_part(count - 1, TAIL_WAITS and sum(history[-1:], ()))
    old = scatters[-2][0]
    while old.step < n - 1:
        old.go()
    if SERIAL_TAIL:
        scatters[-1][0].go(old.last)
    out = back_products(hids, boths, fulls, experts, n)
    if RETURN_AFTER == 1:
        out = after(out, *old.last)
    if RETURN_AFTER == 2:
        scatters[-1][0].go()
        out = after(out, *scatters[-1][0].last)
    returned = exchange(out)
    for _ in range(n - 1):
        for s in scatters[-1]:
            if s.step < n - 1:
                s.go()
    layer_out, grad_tokens, grad_gates = combine(index, target, routing_gates, grad_out, returned, n)
    if COMBINE_EARLY:
        for s in scatters[-1]:
            s.last = tuple(after(x, layer_out) for x in s.last)
    grads = [[s.result() for s in group] for group in scatters]
    stacked = []
    for k in range(3):
        pieces = []
        for s, g in zip(spans, grads):
            f = s.stop - s.start
            pieces.append(
                g[k // 2][:, (k % 2) * f : (k % 2 + 1) * f] if len(g) == 2 else g[0][:, k * f : (k + 1) * f]
            )
        stacked.append(jnp.concatenate(pieces, axis=1)[None])
    return (layer_out, grad_tokens, grad_gates, *stacked)


EARLY = False
WEIGHT = 1 << 34
COMBINE_EARLY = False
WEIGHT = 1 << 34
RETURN_AFTER = 1
DISPATCH_AFTER_PACK = True
EXCHANGE_AFTER_GATHER = False
GATHER_AFTER_PART = True
TAIL_WAITS = True
SERIAL_TAIL = False
LAG = 1


def solution(mesh):
    in_specs = (P(("dp", "expert"), None),) * 5 + (P("expert", "dp", None),) * 3
    out_specs = (P(("dp", "expert"), None),) * 3 + (P("expert", "dp", None),) * 3
    return jax.shard_map(
        on_device, mesh=mesh, in_specs=in_specs, out_specs=out_specs, check_vma=False
    )
```

```python
import functools

import jax
import jax.numpy as jnp
from jax import lax
from jax.experimental import pallas as pl
from jax.experimental.pallas import tpu as pltpu
from jax.sharding import PartitionSpec as P

UNITS = (2, 2, 2)
BF16 = jnp.bfloat16
F32 = jnp.float32
VMEM_LIMIT = 18 * 2**20
WHOLE = pl.BlockSpec(memory_space=pltpu.VMEM)
SCALAR = pl.BlockSpec(memory_space=pltpu.SMEM)


def dot(a, b, ca, cb):
    return lax.dot_general(a, b, (((ca,), (cb,)), ((), ())), preferred_element_type=F32)


def call(body, name, out_shape, in_specs, flops, moved, **extra):
    return pl.pallas_call(
        body,
        name=name,
        out_shape=out_shape,
        in_specs=in_specs,
        compiler_params=pltpu.CompilerParams(vmem_limit_bytes=VMEM_LIMIT),
        cost_estimate=pl.CostEstimate(flops=flops, bytes_accessed=moved, transcendentals=0),
        **extra,
    )


def after(x, *done):
    return lax.optimization_barrier((x, *done))[0] if done else x


def dispatch_body(n, index_ref, target_ref, gates_ref, tokens_ref, grad_ref, out_ref):
    experts, cap = out_ref.shape[0], out_ref.shape[1] // 2
    top_k, tok_dev = target_ref.shape
    feat = tokens_ref.shape[1] // n
    slots = experts * cap
    slot = lax.broadcasted_iota(jnp.int32, (slots, tok_dev), 0)
    pick = jnp.zeros((slots, tok_dev), F32)
    gate = jnp.zeros((slots, 1), F32)
    for k in range(top_k):
        hit = slot == target_ref[k : k + 1, :]
        pick = pick + jnp.where(hit, 1.0, 0.0)
        gate = gate + jnp.sum(jnp.where(hit, gates_ref[k : k + 1, :], 0.0), axis=1, keepdims=True)
    pick = pick.astype(BF16)
    for m in range(n):
        here = slice(m * feat, (m + 1) * feat)
        from_ = pl.ds(pl.multiple_of(lax.rem(index_ref[0] + m, n) * feat, 128), feat)
        rows = dot(pick, tokens_ref[:, from_], 1, 0).astype(BF16)
        grows = (dot(pick, grad_ref[:, from_], 1, 0) * gate).astype(BF16)
        out_ref[:, :cap, here] = rows.reshape(experts, cap, feat)
        out_ref[:, cap:, here] = grows.reshape(experts, cap, feat)


def dispatch(index, target, gates, tokens, grad_out, experts, cap, n):
    width = tokens.shape[1]
    return call(
        functools.partial(dispatch_body, n),
        "dispatch",
        jax.ShapeDtypeStruct((experts, 2 * cap, width), BF16),
        [SCALAR, WHOLE, WHOLE, WHOLE, WHOLE],
        4 * experts * cap * tokens.shape[0] * width,
        4 * (experts * cap + tokens.shape[0]) * width,
        out_specs=WHOLE,
    )(index, target, gates, tokens, grad_out)


def part_body(n, index_ref, rows_ref, *refs):
    own, above, below = refs[0], refs[1:n], refs[n : 2 * n - 1]
    full_ref, hid_ref, both_ref = refs[2 * n - 1 : 2 * n + 2]
    terms, sems = refs[2 * n + 2 : -1], refs[-1]
    feat, three = own.shape
    f = three // 3
    experts, cap = rows_ref.shape[0], rows_ref.shape[1] // 2
    slots = experts * cap

    def fetch(shard, m):
        return pltpu.make_async_copy(shard, full_ref.at[m * feat : (m + 1) * feat], sems.at[m])

    fetch(own, 0).start()
    for m in range(1, n):
        inside = index_ref[0] + m < n

        @pl.when(inside)
        def _():
            fetch(above[m - 1], m).start()

        @pl.when(jnp.logical_not(inside))
        def _():
            fetch(below[n - m - 1], m).start()

    for m in range(n):
        fetch(own, m).wait()
    group = max(1, 128 // cap)
    tile = group * cap

    def forward(t, carry):
        at = pl.ds(pl.multiple_of(t * tile, tile), tile)
        of = pl.ds(t * group, group)
        pre = dot(rows_ref[of, :cap, :].reshape(tile, -1), full_ref[:, : 2 * f], 1, 0)
        gate_pre, up_pre = pre[:, :f], pre[:, f:]
        down_back = dot(rows_ref[of, cap:, :].reshape(tile, -1), full_ref[:, 2 * f :], 1, 0)
        sig = jax.nn.sigmoid(gate_pre)
        active = gate_pre * sig
        hid_ref[at, :] = (active * up_pre).astype(BF16)
        slope = sig * (1.0 + gate_pre * (1.0 - sig))
        both_ref[at, :f] = (down_back * up_pre * slope).astype(BF16)
        both_ref[at, f:] = (down_back * active).astype(BF16)
        return carry

    lax.fori_loop(0, slots // tile, forward, 0)
    for m in range(n):
        cols = slice(m * feat, (m + 1) * feat)
        rows = rows_ref[:, :cap, cols].reshape(slots, feat)
        grows = rows_ref[:, cap:, cols].reshape(slots, feat)
        terms[m][:, : 2 * f] = dot(rows, both_ref[...], 0, 0).astype(BF16)
        terms[m][:, 2 * f :] = dot(grows, hid_ref[...], 0, 0).astype(BF16)


def part(index, rows, own, above, below, n):
    feat, three = own.shape
    experts, double, width = rows.shape
    slots = experts * double // 2
    f = three // 3
    sds = jax.ShapeDtypeStruct
    out_shape = [sds((width, three), BF16), sds((slots, f), BF16), sds((slots, 2 * f), BF16)]
    out_shape += [sds((feat, three), BF16)] * n
    res = call(
        functools.partial(part_body, n),
        "part",
        out_shape,
        [SCALAR, WHOLE] + [pl.BlockSpec(memory_space=pltpu.HBM)] * (2 * n - 1),
        12 * slots * width * f,
        2 * (2 * slots * width + 3 * width * three),
        out_specs=[WHOLE] * len(out_shape),
        scratch_shapes=[pltpu.SemaphoreType.DMA((n,))],
    )(index, rows, own, *above, *below)
    return res[0], res[1], res[2], list(res[3:])


def touch_body(index_ref, *refs):
    refs[-1][0] = index_ref[0]


def touch(index, arrays, weight):
    return call(
        touch_body,
        "touch",
        jax.ShapeDtypeStruct(index.shape, index.dtype),
        [SCALAR] + [pl.BlockSpec(memory_space=pl.ANY)] * len(arrays),
        weight,
        0,
        out_specs=SCALAR,
    )(index, *arrays)


def back_body(count, cap, *refs):
    hids, boths, fulls = refs[:count], refs[count : 2 * count], refs[2 * count : 3 * count]
    out_ref = refs[3 * count]
    experts, _, feat = out_ref.shape
    out = back = None
    for hid, both, full in zip(hids, boths, fulls):
        f = hid.shape[1]
        o = dot(hid[...], full[:, 2 * f :], 1, 1)
        b = dot(both[...], full[:, : 2 * f], 1, 1)
        out, back = (o, b) if out is None else (out + o, back + b)
    out_ref[:, :cap, :] = out.astype(BF16).reshape(experts, cap, feat)
    out_ref[:, cap:, :] = back.astype(BF16).reshape(experts, cap, feat)


def back_products(hids, boths, fulls, experts, n):
    count = len(hids)
    slots = hids[0].shape[0]
    cap = slots // experts
    width = fulls[0].shape[0]
    feat = width // n
    ffn = sum(h.shape[1] for h in hids)
    return pl.pallas_call(
        functools.partial(back_body, count, cap),
        name="back_products",
        out_shape=pltpu.HBM((experts, 2 * cap, width), BF16),
        grid=(n,),
        in_specs=[pl.BlockSpec(x.shape, lambda m: (0, 0)) for x in (*hids, *boths)]
        + [pl.BlockSpec((feat, x.shape[1]), lambda m: (m, 0)) for x in fulls],
        out_specs=pl.BlockSpec((experts, 2 * cap, feat), lambda m: (0, 0, m)),
        compiler_params=pltpu.CompilerParams(vmem_limit_bytes=VMEM_LIMIT),
        cost_estimate=pl.CostEstimate(
            flops=6 * slots * width * ffn,
            bytes_accessed=2 * (3 * ffn * width + 2 * slots * width),
            transcendentals=0,
        ),
    )(*hids, *boths, *fulls)


def combine_body(n, index_ref, target_ref, gates_ref, grad_ref, rows_ref, out_ref, dtok_ref, dgate_ref):
    tok_dev, top_k = target_ref.shape
    experts, cap = rows_ref.shape[0], rows_ref.shape[1] // 2
    slots = experts * cap
    feat = rows_ref.shape[2] // n
    slot = lax.broadcasted_iota(jnp.int32, (tok_dev, slots), 1)
    hits = [jnp.where(slot == target_ref[:, k : k + 1], 1.0, 0.0) for k in range(top_k)]
    either = sum(hits).astype(BF16)
    hits = [h.astype(BF16) for h in hits]
    sums = [jnp.zeros((tok_dev, 1), F32) for _ in range(top_k)]
    for m in range(n):
        here = slice(m * feat, (m + 1) * feat)
        to = pl.ds(pl.multiple_of(lax.rem(index_ref[0] + m, n) * feat, 128), feat)
        total = jnp.zeros((tok_dev, feat), F32)
        grad = grad_ref[:, to].astype(F32)
        rows = rows_ref[:, :cap, here].reshape(slots, feat)
        for k in range(top_k):
            picked = dot(hits[k], rows, 1, 0)
            total = total + picked * gates_ref[:, k : k + 1]
            sums[k] = sums[k] + jnp.sum(picked * grad, axis=1, keepdims=True)
        out_ref[:, to] = total.astype(BF16)
        dtok_ref[:, to] = dot(either, rows_ref[:, cap:, here].reshape(slots, feat), 1, 0).astype(BF16)
    for k in range(top_k):
        dgate_ref[k : k + 1, :] = jnp.broadcast_to(sums[k], (tok_dev, 128)).T[:1, :]


def combine(index, target, gates, grad_out, rows, n):
    shape = jax.ShapeDtypeStruct(grad_out.shape, BF16)
    return call(
        functools.partial(combine_body, n),
        "combine",
        [shape, shape, jax.ShapeDtypeStruct(gates.shape[::-1], F32)],
        [SCALAR, WHOLE, WHOLE, WHOLE, WHOLE],
        3 * rows.shape[0] * rows.shape[1] * grad_out.size,
        2 * (rows.size + 3 * grad_out.size),
        out_specs=[WHOLE, WHOLE, WHOLE],
    )(index, target, gates, grad_out, rows)


def gather_step(step, n, up, down):
    return (
        lax.ppermute(up, "dp", [(j, j + 1) for j in range(step - 1, n - 1)]),
        lax.ppermute(down, "dp", [(j, j - 1) for j in range(n - step, 0, -1)]),
    )


def scatter_step(step, n, up, down):
    return (
        lax.ppermute(up, "dp", [(j, j + 1) for j in range(step)]),
        lax.ppermute(down, "dp", [(j, j - 1) for j in range(n - 1, n - 1 - step, -1)]),
    )


def add(a, b):
    return (a.astype(F32) + b.astype(F32)).astype(BF16)


def exchange(rows):
    return lax.all_to_all(rows, "expert", split_axis=0, concat_axis=0, tiled=True)


class Gather:
    def __init__(self, own, n):
        self.own, self.n, self.step = own, n, 0
        self.last = (own, own)
        self.below, self.above = [], []

    def go(self, waits=()):
        self.step += 1
        up, down = (after(x, *waits) for x in self.last)
        self.last = gather_step(self.step, self.n, up, down)
        self.below.append(self.last[0])
        self.above.append(self.last[1])


class Scatter:
    def __init__(self, terms, n):
        self.terms, self.n, self.step = terms, n, 0
        self.last = ()

    def go(self, waits=()):
        terms, n, step = self.terms, self.n, self.step
        if step:
            up, down = add(self.last[0], terms[n - 1 - step]), add(self.last[1], terms[step + 1])
        else:
            up, down = terms[n - 1], terms[1]
        self.step += 1
        self.last = scatter_step(self.step, n, after(up, *waits), after(down, *waits))

    def result(self):
        up, down = self.last
        return (up.astype(F32) + down.astype(F32) + self.terms[0].astype(F32)).astype(BF16)


def on_device(tokens, expert_ids, slot_index, routing_gates, grad_out, w_gate, w_up, w_down):
    tok_dev, top_k = expert_ids.shape
    experts = lax.axis_size("expert")
    n = lax.axis_size("dp")
    index = lax.axis_index("dp").astype(jnp.int32).reshape(1)
    capacity = 2 * tok_dev * top_k // experts
    unit = w_gate.shape[2] // sum(UNITS)
    edges = [sum(UNITS[:c]) * unit for c in range(len(UNITS) + 1)]
    spans = [slice(a, b) for a, b in zip(edges, edges[1:])]
    count = len(spans)

    owns = [jnp.concatenate([w[0, :, s] for w in (w_gate, w_up, w_down)], axis=1) for s in spans]
    target = expert_ids * capacity + slot_index
    if DISPATCH_AFTER_PACK:
        target = after(target, owns[0])
    sent = dispatch(index, target.T, routing_gates.T, tokens, grad_out, experts, capacity, n)

    fulls, hids, boths = [], [], []
    gathers = [Gather(own, n) for own in owns]
    scatters = []

    def run_part(c, waits=()):
        g = gathers[c]
        ready = touch(index, g.last, WEIGHT) if c == 0 else index
        full, hid, both, terms = part(ready, after(rows, *waits), g.own, g.above, g.below, n)
        fulls.append(full)
        hids.append(hid)
        boths.append(both)
        scatters.append([Scatter(terms, n)])

    gathers[0].go()
    if EXCHANGE_AFTER_GATHER:
        sent = after(sent, *gathers[0].last)
    rows = exchange(sent)
    for _ in range(n - 2):
        gathers[0].go()
    history = [gathers[0].last]
    for c in range(1, count):
        for step in range(1, n):
            if step == 2:
                run_part(c - 1)
            waits = sum(history[-LAG:-LAG + 1 or None], ())
            if step == 1 and c == 1 and EARLY:
                waits = (gathers[0].below[-2], gathers[0].above[-2])
            if step == 2 and GATHER_AFTER_PART:
                waits += (hids[-1],)
            gathers[c].go(waits)
            done = gathers[c].last
            for (s,) in scatters:
                if s.step < n - 1:
                    s.go()
                    done += s.last
            history.append(done)
    run_part(count - 1, TAIL_WAITS and sum(history[-1:], ()))
    old = scatters[-2][0]
    while old.step < n - 1:
        old.go()
    if SERIAL_TAIL:
        scatters[-1][0].go(old.last)
    out = back_products(hids, boths, fulls, experts, n)
    if RETURN_AFTER == 1:
        out = after(out, *old.last)
    if RETURN_AFTER == 2:
        scatters[-1][0].go()
        out = after(out, *scatters[-1][0].last)
    returned = exchange(out)
    for _ in range(n - 1):
        for s in scatters[-1]:
            if s.step < n - 1:
                s.go()
    layer_out, grad_tokens, grad_gates = combine(index, target, routing_gates, grad_out, returned, n)
    if COMBINE_EARLY:
        for s in scatters[-1]:
            s.last = tuple(after(x, layer_out) for x in s.last)
    grads = [[s.result() for s in group] for group in scatters]
    stacked = []
    for k in range(3):
        pieces = []
        for s, g in zip(spans, grads):
            f = s.stop - s.start
            pieces.append(
                g[k // 2][:, (k % 2) * f : (k % 2 + 1) * f] if len(g) == 2 else g[0][:, k * f : (k + 1) * f]
            )
        stacked.append(jnp.concatenate(pieces, axis=1)[None])
    return (layer_out, grad_tokens, grad_gates.T, *stacked)


EARLY = False
WEIGHT = 1 << 34
COMBINE_EARLY = False
WEIGHT = 1 << 34
RETURN_AFTER = 1
DISPATCH_AFTER_PACK = True
EXCHANGE_AFTER_GATHER = False
GATHER_AFTER_PART = False
TAIL_WAITS = True
SERIAL_TAIL = False
LAG = 1


def solution(mesh):
    in_specs = (P(("dp", "expert"), None),) * 5 + (P("expert", "dp", None),) * 3
    out_specs = (P(("dp", "expert"), None),) * 3 + (P("expert", "dp", None),) * 3
    return jax.shard_map(
        on_device, mesh=mesh, in_specs=in_specs, out_specs=out_specs, check_vma=False
    )
```

```python
import functools

import jax
import jax.numpy as jnp
from jax import lax
from jax.experimental import pallas as pl
from jax.experimental.pallas import tpu as pltpu
from jax.sharding import PartitionSpec as P

UNITS = (2, 2, 2)
BF16 = jnp.bfloat16
F32 = jnp.float32
VMEM_LIMIT = 18 * 2**20
WHOLE = pl.BlockSpec(memory_space=pltpu.VMEM)
SCALAR = pl.BlockSpec(memory_space=pltpu.SMEM)


def dot(a, b, ca, cb):
    return lax.dot_general(a, b, (((ca,), (cb,)), ((), ())), preferred_element_type=F32)


def call(body, name, out_shape, in_specs, flops, moved, **extra):
    return pl.pallas_call(
        body,
        name=name,
        out_shape=out_shape,
        in_specs=in_specs,
        compiler_params=pltpu.CompilerParams(vmem_limit_bytes=VMEM_LIMIT),
        cost_estimate=pl.CostEstimate(flops=flops, bytes_accessed=moved, transcendentals=0),
        **extra,
    )


def after(x, *done):
    return lax.optimization_barrier((x, *done))[0] if done else x


def dispatch_body(n, index_ref, target_ref, gates_ref, tokens_ref, grad_ref, out_ref):
    experts, cap = out_ref.shape[0], out_ref.shape[1] // 2
    top_k, tok_dev = target_ref.shape
    feat = tokens_ref.shape[1] // n
    slots = experts * cap
    slot = lax.broadcasted_iota(jnp.int32, (slots, tok_dev), 0)
    pick = jnp.zeros((slots, tok_dev), F32)
    gate = jnp.zeros((slots, 1), F32)
    for k in range(top_k):
        hit = slot == target_ref[k : k + 1, :]
        pick = pick + jnp.where(hit, 1.0, 0.0)
        gate = gate + jnp.sum(jnp.where(hit, gates_ref[k : k + 1, :], 0.0), axis=1, keepdims=True)
    pick = pick.astype(BF16)
    for m in range(n):
        here = slice(m * feat, (m + 1) * feat)
        from_ = pl.ds(pl.multiple_of(lax.rem(index_ref[0] + m, n) * feat, 128), feat)
        rows = dot(pick, tokens_ref[:, from_], 1, 0).astype(BF16)
        grows = (dot(pick, grad_ref[:, from_], 1, 0) * gate).astype(BF16)
        out_ref[:, :cap, here] = rows.reshape(experts, cap, feat)
        out_ref[:, cap:, here] = grows.reshape(experts, cap, feat)


def dispatch(index, target, gates, tokens, grad_out, experts, cap, n):
    width = tokens.shape[1]
    return call(
        functools.partial(dispatch_body, n),
        "dispatch",
        jax.ShapeDtypeStruct((experts, 2 * cap, width), BF16),
        [SCALAR, WHOLE, WHOLE, WHOLE, WHOLE],
        4 * experts * cap * tokens.shape[0] * width,
        4 * (experts * cap + tokens.shape[0]) * width,
        out_specs=WHOLE,
    )(index, target, gates, tokens, grad_out)


def part_body(n, index_ref, rows_ref, *refs):
    own, above, below = refs[0], refs[1:n], refs[n : 2 * n - 1]
    full_ref, hid_ref, both_ref = refs[2 * n - 1 : 2 * n + 2]
    terms, sems = refs[2 * n + 2 : -1], refs[-1]
    feat, three = own.shape
    f = three // 3
    experts, cap = rows_ref.shape[0], rows_ref.shape[1] // 2
    slots = experts * cap

    def fetch(shard, m):
        return pltpu.make_async_copy(shard, full_ref.at[m * feat : (m + 1) * feat], sems.at[m])

    fetch(own, 0).start()
    for m in range(1, n):
        inside = index_ref[0] + m < n

        @pl.when(inside)
        def _():
            fetch(above[m - 1], m).start()

        @pl.when(jnp.logical_not(inside))
        def _():
            fetch(below[n - m - 1], m).start()

    for m in range(n):
        fetch(own, m).wait()
    group = max(1, 128 // cap)
    tile = group * cap

    def forward(t, carry):
        at = pl.ds(pl.multiple_of(t * tile, tile), tile)
        of = pl.ds(t * group, group)
        pre = dot(rows_ref[of, :cap, :].reshape(tile, -1), full_ref[:, : 2 * f], 1, 0)
        gate_pre, up_pre = pre[:, :f], pre[:, f:]
        down_back = dot(rows_ref[of, cap:, :].reshape(tile, -1), full_ref[:, 2 * f :], 1, 0)
        sig = jax.nn.sigmoid(gate_pre)
        active = gate_pre * sig
        hid_ref[at, :] = (active * up_pre).astype(BF16)
        slope = sig * (1.0 + gate_pre * (1.0 - sig))
        both_ref[at, :f] = (down_back * up_pre * slope).astype(BF16)
        both_ref[at, f:] = (down_back * active).astype(BF16)
        return carry

    lax.fori_loop(0, slots // tile, forward, 0)
    for m in range(n):
        cols = slice(m * feat, (m + 1) * feat)
        rows = rows_ref[:, :cap, cols].reshape(slots, feat)
        grows = rows_ref[:, cap:, cols].reshape(slots, feat)
        terms[m][:, : 2 * f] = dot(rows, both_ref[...], 0, 0).astype(BF16)
        terms[m][:, 2 * f :] = dot(grows, hid_ref[...], 0, 0).astype(BF16)


def part(index, rows, own, above, below, n):
    feat, three = own.shape
    experts, double, width = rows.shape
    slots = experts * double // 2
    f = three // 3
    sds = jax.ShapeDtypeStruct
    out_shape = [sds((width, three), BF16), sds((slots, f), BF16), sds((slots, 2 * f), BF16)]
    out_shape += [sds((feat, three), BF16)] * n
    res = call(
        functools.partial(part_body, n),
        "part",
        out_shape,
        [SCALAR, WHOLE] + [pl.BlockSpec(memory_space=pltpu.HBM)] * (2 * n - 1),
        12 * slots * width * f,
        2 * (2 * slots * width + 3 * width * three),
        out_specs=[WHOLE] * len(out_shape),
        scratch_shapes=[pltpu.SemaphoreType.DMA((n,))],
    )(index, rows, own, *above, *below)
    return res[0], res[1], res[2], list(res[3:])


def touch_body(index_ref, *refs):
    refs[-1][0] = index_ref[0]


def touch(index, arrays, weight):
    return call(
        touch_body,
        "touch",
        jax.ShapeDtypeStruct(index.shape, index.dtype),
        [SCALAR] + [pl.BlockSpec(memory_space=pl.ANY)] * len(arrays),
        weight,
        0,
        out_specs=SCALAR,
    )(index, *arrays)


def back_body(count, cap, *refs):
    hids, boths, fulls = refs[:count], refs[count : 2 * count], refs[2 * count : 3 * count]
    out_ref = refs[3 * count]
    experts, _, feat = out_ref.shape
    out = back = None
    for hid, both, full in zip(hids, boths, fulls):
        f = hid.shape[1]
        o = dot(hid[...], full[:, 2 * f :], 1, 1)
        b = dot(both[...], full[:, : 2 * f], 1, 1)
        out, back = (o, b) if out is None else (out + o, back + b)
    out_ref[:, :cap, :] = out.astype(BF16).reshape(experts, cap, feat)
    out_ref[:, cap:, :] = back.astype(BF16).reshape(experts, cap, feat)


def back_products(hids, boths, fulls, experts, n):
    count = len(hids)
    slots = hids[0].shape[0]
    cap = slots // experts
    width = fulls[0].shape[0]
    feat = width // n
    ffn = sum(h.shape[1] for h in hids)
    return pl.pallas_call(
        functools.partial(back_body, count, cap),
        name="back_products",
        out_shape=pltpu.HBM((experts, 2 * cap, width), BF16),
        grid=(n,),
        in_specs=[pl.BlockSpec(x.shape, lambda m: (0, 0)) for x in (*hids, *boths)]
        + [pl.BlockSpec((feat, x.shape[1]), lambda m: (m, 0)) for x in fulls],
        out_specs=pl.BlockSpec((experts, 2 * cap, feat), lambda m: (0, 0, m)),
        compiler_params=pltpu.CompilerParams(vmem_limit_bytes=VMEM_LIMIT),
        cost_estimate=pl.CostEstimate(
            flops=6 * slots * width * ffn,
            bytes_accessed=2 * (3 * ffn * width + 2 * slots * width),
            transcendentals=0,
        ),
    )(*hids, *boths, *fulls)


def combine_body(n, index_ref, target_ref, gates_ref, grad_ref, rows_ref, out_ref, dtok_ref, dgate_ref):
    tok_dev, top_k = target_ref.shape
    experts, cap = rows_ref.shape[0], rows_ref.shape[1] // 2
    slots = experts * cap
    feat = rows_ref.shape[2] // n
    slot = lax.broadcasted_iota(jnp.int32, (tok_dev, slots), 1)
    hits = [jnp.where(slot == target_ref[:, k : k + 1], 1.0, 0.0) for k in range(top_k)]
    either = sum(hits).astype(BF16)
    hits = [h.astype(BF16) for h in hits]
    sums = [jnp.zeros((tok_dev, 1), F32) for _ in range(top_k)]
    for m in range(n):
        here = slice(m * feat, (m + 1) * feat)
        to = pl.ds(pl.multiple_of(lax.rem(index_ref[0] + m, n) * feat, 128), feat)
        total = jnp.zeros((tok_dev, feat), F32)
        grad = grad_ref[:, to].astype(F32)
        rows = rows_ref[:, :cap, here].reshape(slots, feat)
        for k in range(top_k):
            picked = dot(hits[k], rows, 1, 0)
            total = total + picked * gates_ref[:, k : k + 1]
            sums[k] = sums[k] + jnp.sum(picked * grad, axis=1, keepdims=True)
        out_ref[:, to] = total.astype(BF16)
        dtok_ref[:, to] = dot(either, rows_ref[:, cap:, here].reshape(slots, feat), 1, 0).astype(BF16)
    for k in range(top_k):
        dgate_ref[k : k + 1, :] = jnp.broadcast_to(sums[k], (tok_dev, 128)).T[:1, :]


def combine(index, target, gates, grad_out, rows, n):
    shape = jax.ShapeDtypeStruct(grad_out.shape, BF16)
    return call(
        functools.partial(combine_body, n),
        "combine",
        [shape, shape, jax.ShapeDtypeStruct(gates.shape[::-1], F32)],
        [SCALAR, WHOLE, WHOLE, WHOLE, WHOLE],
        3 * rows.shape[0] * rows.shape[1] * grad_out.size,
        2 * (rows.size + 3 * grad_out.size),
        out_specs=[WHOLE, WHOLE, WHOLE],
    )(index, target, gates, grad_out, rows)


def gather_step(step, n, up, down):
    return (
        lax.ppermute(up, "dp", [(j, j + 1) for j in range(step - 1, n - 1)]),
        lax.ppermute(down, "dp", [(j, j - 1) for j in range(n - step, 0, -1)]),
    )


def scatter_step(step, n, up, down):
    return (
        lax.ppermute(up, "dp", [(j, j + 1) for j in range(step)]),
        lax.ppermute(down, "dp", [(j, j - 1) for j in range(n - 1, n - 1 - step, -1)]),
    )


def add(a, b):
    return (a.astype(F32) + b.astype(F32)).astype(BF16)


def exchange(rows):
    return lax.all_to_all(rows, "expert", split_axis=0, concat_axis=0, tiled=True)


class Gather:
    def __init__(self, own, n):
        self.own, self.n, self.step = own, n, 0
        self.last = (own, own)
        self.below, self.above = [], []

    def go(self, waits=()):
        self.step += 1
        up, down = (after(x, *waits) for x in self.last)
        self.last = gather_step(self.step, self.n, up, down)
        self.below.append(self.last[0])
        self.above.append(self.last[1])


class Scatter:
    def __init__(self, terms, n):
        self.terms, self.n, self.step = terms, n, 0
        self.last = ()

    def go(self, waits=()):
        terms, n, step = self.terms, self.n, self.step
        if step:
            up, down = add(self.last[0], terms[n - 1 - step]), add(self.last[1], terms[step + 1])
        else:
            up, down = terms[n - 1], terms[1]
        self.step += 1
        self.last = scatter_step(self.step, n, after(up, *waits), after(down, *waits))

    def result(self):
        up, down = self.last
        return (up.astype(F32) + down.astype(F32) + self.terms[0].astype(F32)).astype(BF16)


def on_device(tokens, expert_ids, slot_index, routing_gates, grad_out, w_gate, w_up, w_down):
    tok_dev, top_k = expert_ids.shape
    experts = lax.axis_size("expert")
    n = lax.axis_size("dp")
    index = lax.axis_index("dp").astype(jnp.int32).reshape(1)
    capacity = 2 * tok_dev * top_k // experts
    unit = w_gate.shape[2] // sum(UNITS)
    edges = [sum(UNITS[:c]) * unit for c in range(len(UNITS) + 1)]
    spans = [slice(a, b) for a, b in zip(edges, edges[1:])]
    count = len(spans)

    def pack(span, weights):
        return jnp.concatenate([w[0, :, span] for w in weights], axis=1)

    weights = (w_gate, w_up, w_down)
    own = pack(spans[0], weights)
    target = expert_ids * capacity + slot_index
    if DISPATCH_AFTER_PACK:
        target = after(target, own)
    sent = dispatch(index, target.T, routing_gates.T, tokens, grad_out, experts, capacity, n)

    fulls, hids, boths = [], [], []
    gathers = [Gather(own, n)]
    scatters = []

    def run_part(c, waits=()):
        g = gathers[c]
        ready = touch(index, g.last, WEIGHT) if c == 0 else index
        full, hid, both, terms = part(ready, after(rows, *waits), g.own, g.above, g.below, n)
        fulls.append(full)
        hids.append(hid)
        boths.append(both)
        scatters.append([Scatter(terms, n)])

    gathers[0].go()
    weights = [after(w, *gathers[0].last) for w in weights]
    gathers += [Gather(pack(span, weights), n) for span in spans[1:]]
    if EXCHANGE_AFTER_GATHER:
        sent = after(sent, *gathers[0].last)
    rows = exchange(sent)
    for _ in range(n - 2):
        gathers[0].go()
    history = [gathers[0].last]
    for c in range(1, count):
        for step in range(1, n):
            if step == 2:
                run_part(c - 1)
            waits = sum(history[-LAG:-LAG + 1 or None], ())
            if step == 1 and c == 1 and EARLY:
                waits = (gathers[0].below[-2], gathers[0].above[-2])
            if step == 2 and GATHER_AFTER_PART:
                waits += (hids[-1],)
            gathers[c].go(waits)
            done = gathers[c].last
            for (s,) in scatters:
                if s.step < n - 1:
                    s.go()
                    done += s.last
            history.append(done)
    run_part(count - 1, TAIL_WAITS and sum(history[-1:], ()))
    old = scatters[-2][0]
    while old.step < n - 1:
        old.go()
    if SERIAL_TAIL:
        scatters[-1][0].go(old.last)
    out = back_products(hids, boths, fulls, experts, n)
    if RETURN_AFTER == 1:
        out = after(out, *old.last)
    if RETURN_AFTER == 2:
        scatters[-1][0].go()
        out = after(out, *scatters[-1][0].last)
    returned = exchange(out)
    for _ in range(n - 1):
        for s in scatters[-1]:
            if s.step < n - 1:
                s.go()
    layer_out, grad_tokens, grad_gates = combine(index, target, routing_gates, grad_out, returned, n)
    if COMBINE_EARLY:
        for s in scatters[-1]:
            s.last = tuple(after(x, layer_out) for x in s.last)
    grads = [[s.result() for s in group] for group in scatters]
    stacked = []
    for k in range(3):
        pieces = []
        for s, g in zip(spans, grads):
            f = s.stop - s.start
            pieces.append(
                g[k // 2][:, (k % 2) * f : (k % 2 + 1) * f] if len(g) == 2 else g[0][:, k * f : (k + 1) * f]
            )
        stacked.append(jnp.concatenate(pieces, axis=1)[None])
    return (layer_out, grad_tokens, grad_gates.T, *stacked)


EARLY = False
WEIGHT = 1 << 34
COMBINE_EARLY = False
WEIGHT = 1 << 34
RETURN_AFTER = 1
DISPATCH_AFTER_PACK = True
EXCHANGE_AFTER_GATHER = False
GATHER_AFTER_PART = False
TAIL_WAITS = True
SERIAL_TAIL = False
LAG = 1


def solution(mesh):
    in_specs = (P(("dp", "expert"), None),) * 5 + (P("expert", "dp", None),) * 3
    out_specs = (P(("dp", "expert"), None),) * 3 + (P("expert", "dp", None),) * 3
    return jax.shard_map(
        on_device, mesh=mesh, in_specs=in_specs, out_specs=out_specs, check_vma=False
    )
```

```python
import functools

import jax
import jax.numpy as jnp
from jax import lax
from jax.experimental import pallas as pl
from jax.experimental.pallas import tpu as pltpu
from jax.sharding import PartitionSpec as P

UNITS = (2, 2, 2)
BF16 = jnp.bfloat16
F32 = jnp.float32
VMEM_LIMIT = 18 * 2**20
WHOLE = pl.BlockSpec(memory_space=pltpu.VMEM)
SCALAR = pl.BlockSpec(memory_space=pltpu.SMEM)


def dot(a, b, ca, cb):
    return lax.dot_general(a, b, (((ca,), (cb,)), ((), ())), preferred_element_type=F32)


def call(body, name, out_shape, in_specs, flops, moved, **extra):
    return pl.pallas_call(
        body,
        name=name,
        out_shape=out_shape,
        in_specs=in_specs,
        compiler_params=pltpu.CompilerParams(vmem_limit_bytes=VMEM_LIMIT),
        cost_estimate=pl.CostEstimate(flops=flops, bytes_accessed=moved, transcendentals=0),
        **extra,
    )


def after(x, *done):
    return lax.optimization_barrier((x, *done))[0] if done else x


def dispatch_body(n, index_ref, target_ref, gates_ref, tokens_ref, grad_ref, out_ref):
    experts, cap = out_ref.shape[0], out_ref.shape[1] // 2
    top_k, tok_dev = target_ref.shape
    feat = tokens_ref.shape[1] // n
    slots = experts * cap
    slot = lax.broadcasted_iota(jnp.int32, (slots, tok_dev), 0)
    pick = jnp.zeros((slots, tok_dev), F32)
    gate = jnp.zeros((slots, 1), F32)
    for k in range(top_k):
        hit = slot == target_ref[k : k + 1, :]
        pick = pick + jnp.where(hit, 1.0, 0.0)
        gate = gate + jnp.sum(jnp.where(hit, gates_ref[k : k + 1, :], 0.0), axis=1, keepdims=True)
    pick = pick.astype(BF16)
    for m in range(n):
        here = slice(m * feat, (m + 1) * feat)
        from_ = pl.ds(pl.multiple_of(lax.rem(index_ref[0] + m, n) * feat, 128), feat)
        rows = dot(pick, tokens_ref[:, from_], 1, 0).astype(BF16)
        grows = (dot(pick, grad_ref[:, from_], 1, 0) * gate).astype(BF16)
        out_ref[:, :cap, here] = rows.reshape(experts, cap, feat)
        out_ref[:, cap:, here] = grows.reshape(experts, cap, feat)


def dispatch(index, target, gates, tokens, grad_out, experts, cap, n):
    width = tokens.shape[1]
    return call(
        functools.partial(dispatch_body, n),
        "dispatch",
        pltpu.HBM((experts, 2 * cap, width), BF16),
        [SCALAR, WHOLE, WHOLE, WHOLE, WHOLE],
        4 * experts * cap * tokens.shape[0] * width,
        4 * (experts * cap + tokens.shape[0]) * width,
        out_specs=WHOLE,
    )(index, target, gates, tokens, grad_out)


def part_body(n, index_ref, rows_ref, *refs):
    own, above, below = refs[0], refs[1:n], refs[n : 2 * n - 1]
    full_ref, hid_ref, both_ref = refs[2 * n - 1 : 2 * n + 2]
    terms, sems = refs[2 * n + 2 : -1], refs[-1]
    feat, three = own.shape
    f = three // 3
    experts, cap = rows_ref.shape[0], rows_ref.shape[1] // 2
    slots = experts * cap

    def fetch(shard, m):
        return pltpu.make_async_copy(shard, full_ref.at[m * feat : (m + 1) * feat], sems.at[m])

    fetch(own, 0).start()
    for m in range(1, n):
        inside = index_ref[0] + m < n

        @pl.when(inside)
        def _():
            fetch(above[m - 1], m).start()

        @pl.when(jnp.logical_not(inside))
        def _():
            fetch(below[n - m - 1], m).start()

    for m in range(n):
        fetch(own, m).wait()
    group = max(1, 128 // cap)
    tile = group * cap

    def forward(t, carry):
        at = pl.ds(pl.multiple_of(t * tile, tile), tile)
        of = pl.ds(t * group, group)
        pre = dot(rows_ref[of, :cap, :].reshape(tile, -1), full_ref[:, : 2 * f], 1, 0)
        gate_pre, up_pre = pre[:, :f], pre[:, f:]
        down_back = dot(rows_ref[of, cap:, :].reshape(tile, -1), full_ref[:, 2 * f :], 1, 0)
        sig = jax.nn.sigmoid(gate_pre)
        active = gate_pre * sig
        hid_ref[at, :] = (active * up_pre).astype(BF16)
        slope = sig * (1.0 + gate_pre * (1.0 - sig))
        both_ref[at, :f] = (down_back * up_pre * slope).astype(BF16)
        both_ref[at, f:] = (down_back * active).astype(BF16)
        return carry

    lax.fori_loop(0, slots // tile, forward, 0)
    for m in range(n):
        cols = slice(m * feat, (m + 1) * feat)
        rows = rows_ref[:, :cap, cols].reshape(slots, feat)
        grows = rows_ref[:, cap:, cols].reshape(slots, feat)
        terms[m][:, : 2 * f] = dot(rows, both_ref[...], 0, 0).astype(BF16)
        terms[m][:, 2 * f :] = dot(grows, hid_ref[...], 0, 0).astype(BF16)


def part(index, rows, own, above, below, n):
    feat, three = own.shape
    experts, double, width = rows.shape
    slots = experts * double // 2
    f = three // 3
    sds = jax.ShapeDtypeStruct
    out_shape = [sds((width, three), BF16), sds((slots, f), BF16), sds((slots, 2 * f), BF16)]
    out_shape += [sds((feat, three), BF16)] * n
    res = call(
        functools.partial(part_body, n),
        "part",
        out_shape,
        [SCALAR, WHOLE] + [pl.BlockSpec(memory_space=pltpu.HBM)] * (2 * n - 1),
        12 * slots * width * f,
        2 * (2 * slots * width + 3 * width * three),
        out_specs=[WHOLE] * len(out_shape),
        scratch_shapes=[pltpu.SemaphoreType.DMA((n,))],
    )(index, rows, own, *above, *below)
    return res[0], res[1], res[2], list(res[3:])


def touch_body(index_ref, *refs):
    refs[-1][0] = index_ref[0]


def touch(index, arrays, weight):
    return call(
        touch_body,
        "touch",
        jax.ShapeDtypeStruct(index.shape, index.dtype),
        [SCALAR] + [pl.BlockSpec(memory_space=pl.ANY)] * len(arrays),
        weight,
        0,
        out_specs=SCALAR,
    )(index, *arrays)


def back_body(count, cap, *refs):
    hids, boths, fulls = refs[:count], refs[count : 2 * count], refs[2 * count : 3 * count]
    out_ref = refs[3 * count]
    experts, _, feat = out_ref.shape
    out = back = None
    for hid, both, full in zip(hids, boths, fulls):
        f = hid.shape[1]
        o = dot(hid[...], full[:, 2 * f :], 1, 1)
        b = dot(both[...], full[:, : 2 * f], 1, 1)
        out, back = (o, b) if out is None else (out + o, back + b)
    out_ref[:, :cap, :] = out.astype(BF16).reshape(experts, cap, feat)
    out_ref[:, cap:, :] = back.astype(BF16).reshape(experts, cap, feat)


def back_products(hids, boths, fulls, experts, n):
    count = len(hids)
    slots = hids[0].shape[0]
    cap = slots // experts
    width = fulls[0].shape[0]
    feat = width // n
    ffn = sum(h.shape[1] for h in hids)
    return pl.pallas_call(
        functools.partial(back_body, count, cap),
        name="back_products",
        out_shape=pltpu.HBM((experts, 2 * cap, width), BF16),
        grid=(n,),
        in_specs=[pl.BlockSpec(x.shape, lambda m: (0, 0)) for x in (*hids, *boths)]
        + [pl.BlockSpec((feat, x.shape[1]), lambda m: (m, 0)) for x in fulls],
        out_specs=pl.BlockSpec((experts, 2 * cap, feat), lambda m: (0, 0, m)),
        compiler_params=pltpu.CompilerParams(vmem_limit_bytes=VMEM_LIMIT),
        cost_estimate=pl.CostEstimate(
            flops=6 * slots * width * ffn,
            bytes_accessed=2 * (3 * ffn * width + 2 * slots * width),
            transcendentals=0,
        ),
    )(*hids, *boths, *fulls)


def combine_body(n, index_ref, target_ref, gates_ref, grad_ref, rows_ref, out_ref, dtok_ref, dgate_ref):
    tok_dev, top_k = target_ref.shape
    experts, cap = rows_ref.shape[0], rows_ref.shape[1] // 2
    slots = experts * cap
    feat = rows_ref.shape[2] // n
    slot = lax.broadcasted_iota(jnp.int32, (tok_dev, slots), 1)
    hits = [jnp.where(slot == target_ref[:, k : k + 1], 1.0, 0.0) for k in range(top_k)]
    either = sum(hits).astype(BF16)
    hits = [h.astype(BF16) for h in hits]
    sums = [jnp.zeros((tok_dev, 1), F32) for _ in range(top_k)]
    for m in range(n):
        here = slice(m * feat, (m + 1) * feat)
        to = pl.ds(pl.multiple_of(lax.rem(index_ref[0] + m, n) * feat, 128), feat)
        total = jnp.zeros((tok_dev, feat), F32)
        grad = grad_ref[:, to].astype(F32)
        rows = rows_ref[:, :cap, here].reshape(slots, feat)
        for k in range(top_k):
            picked = dot(hits[k], rows, 1, 0)
            total = total + picked * gates_ref[:, k : k + 1]
            sums[k] = sums[k] + jnp.sum(picked * grad, axis=1, keepdims=True)
        out_ref[:, to] = total.astype(BF16)
        dtok_ref[:, to] = dot(either, rows_ref[:, cap:, here].reshape(slots, feat), 1, 0).astype(BF16)
    for k in range(top_k):
        dgate_ref[k : k + 1, :] = jnp.broadcast_to(sums[k], (tok_dev, 128)).T[:1, :]


def combine(index, target, gates, grad_out, rows, n):
    shape = jax.ShapeDtypeStruct(grad_out.shape, BF16)
    return call(
        functools.partial(combine_body, n),
        "combine",
        [shape, shape, jax.ShapeDtypeStruct(gates.shape[::-1], F32)],
        [SCALAR, WHOLE, WHOLE, WHOLE, WHOLE],
        3 * rows.shape[0] * rows.shape[1] * grad_out.size,
        2 * (rows.size + 3 * grad_out.size),
        out_specs=[WHOLE, WHOLE, WHOLE],
    )(index, target, gates, grad_out, rows)


def gather_step(step, n, up, down):
    return (
        lax.ppermute(up, "dp", [(j, j + 1) for j in range(step - 1, n - 1)]),
        lax.ppermute(down, "dp", [(j, j - 1) for j in range(n - step, 0, -1)]),
    )


def scatter_step(step, n, up, down):
    return (
        lax.ppermute(up, "dp", [(j, j + 1) for j in range(step)]),
        lax.ppermute(down, "dp", [(j, j - 1) for j in range(n - 1, n - 1 - step, -1)]),
    )


def add(a, b):
    return (a.astype(F32) + b.astype(F32)).astype(BF16)


def exchange(rows):
    return lax.all_to_all(rows, "expert", split_axis=0, concat_axis=0, tiled=True)


class Gather:
    def __init__(self, own, n):
        self.own, self.n, self.step = own, n, 0
        self.last = (own, own)
        self.below, self.above = [], []

    def go(self, waits=()):
        self.step += 1
        up, down = (after(x, *waits) for x in self.last)
        self.last = gather_step(self.step, self.n, up, down)
        self.below.append(self.last[0])
        self.above.append(self.last[1])


class Scatter:
    def __init__(self, terms, n):
        self.terms, self.n, self.step = terms, n, 0
        self.last = ()

    def go(self, waits=()):
        terms, n, step = self.terms, self.n, self.step
        if step:
            up, down = add(self.last[0], terms[n - 1 - step]), add(self.last[1], terms[step + 1])
        else:
            up, down = terms[n - 1], terms[1]
        self.step += 1
        self.last = scatter_step(self.step, n, after(up, *waits), after(down, *waits))

    def result(self):
        up, down = self.last
        return (up.astype(F32) + down.astype(F32) + self.terms[0].astype(F32)).astype(BF16)


def on_device(tokens, expert_ids, slot_index, routing_gates, grad_out, w_gate, w_up, w_down):
    tok_dev, top_k = expert_ids.shape
    experts = lax.axis_size("expert")
    n = lax.axis_size("dp")
    index = lax.axis_index("dp").astype(jnp.int32).reshape(1)
    capacity = 2 * tok_dev * top_k // experts
    unit = w_gate.shape[2] // sum(UNITS)
    edges = [sum(UNITS[:c]) * unit for c in range(len(UNITS) + 1)]
    spans = [slice(a, b) for a, b in zip(edges, edges[1:])]
    count = len(spans)

    def pack(span, weights):
        return jnp.concatenate([w[0, :, span] for w in weights], axis=1)

    weights = (w_gate, w_up, w_down)
    own = pack(spans[0], weights)
    target = expert_ids * capacity + slot_index
    if DISPATCH_AFTER_PACK:
        target = after(target, own)
    sent = dispatch(index, target.T, routing_gates.T, tokens, grad_out, experts, capacity, n)

    fulls, hids, boths = [], [], []
    gathers = [Gather(own, n)]
    scatters = []

    def run_part(c, waits=()):
        g = gathers[c]
        ready = touch(index, g.last, WEIGHT) if c == 0 else index
        full, hid, both, terms = part(ready, after(rows, *waits), g.own, g.above, g.below, n)
        fulls.append(full)
        hids.append(hid)
        boths.append(both)
        scatters.append([Scatter(terms, n)])

    gathers[0].go()
    weights = [after(w, *gathers[0].last) for w in weights]
    gathers += [Gather(pack(span, weights), n) for span in spans[1:]]
    if EXCHANGE_AFTER_GATHER:
        sent = after(sent, *gathers[0].last)
    rows = exchange(sent)
    for _ in range(n - 2):
        gathers[0].go()
    history = [gathers[0].last]
    for c in range(1, count):
        for step in range(1, n):
            if step == 2:
                run_part(c - 1)
            waits = sum(history[-LAG:-LAG + 1 or None], ())
            if step == 1 and c == 1 and EARLY:
                waits = (gathers[0].below[-2], gathers[0].above[-2])
            if step == 2 and GATHER_AFTER_PART:
                waits += (hids[-1],)
            gathers[c].go(waits)
            done = gathers[c].last
            for (s,) in scatters:
                if s.step < n - 1:
                    s.go()
                    done += s.last
            history.append(done)
    run_part(count - 1, TAIL_WAITS and sum(history[-1:], ()))
    old = scatters[-2][0]
    while old.step < n - 1:
        old.go()
    if SERIAL_TAIL:
        scatters[-1][0].go(old.last)
    out = back_products(hids, boths, fulls, experts, n)
    if RETURN_AFTER == 1:
        out = after(out, *old.last)
    if RETURN_AFTER == 2:
        scatters[-1][0].go()
        out = after(out, *scatters[-1][0].last)
    returned = exchange(out)
    for _ in range(n - 1):
        for s in scatters[-1]:
            if s.step < n - 1:
                s.go()
    layer_out, grad_tokens, grad_gates = combine(index, target, routing_gates, grad_out, returned, n)
    if COMBINE_EARLY:
        for s in scatters[-1]:
            s.last = tuple(after(x, layer_out) for x in s.last)
    grads = [[s.result() for s in group] for group in scatters]
    stacked = []
    for k in range(3):
        pieces = []
        for s, g in zip(spans, grads):
            f = s.stop - s.start
            pieces.append(
                g[k // 2][:, (k % 2) * f : (k % 2 + 1) * f] if len(g) == 2 else g[0][:, k * f : (k + 1) * f]
            )
        stacked.append(jnp.concatenate(pieces, axis=1)[None])
    return (layer_out, grad_tokens, grad_gates.T, *stacked)


EARLY = False
WEIGHT = 1 << 34
COMBINE_EARLY = False
WEIGHT = 1 << 34
RETURN_AFTER = 1
DISPATCH_AFTER_PACK = True
EXCHANGE_AFTER_GATHER = False
GATHER_AFTER_PART = False
TAIL_WAITS = True
SERIAL_TAIL = False
LAG = 1


def solution(mesh):
    in_specs = (P(("dp", "expert"), None),) * 5 + (P("expert", "dp", None),) * 3
    out_specs = (P(("dp", "expert"), None),) * 3 + (P("expert", "dp", None),) * 3
    return jax.shard_map(
        on_device, mesh=mesh, in_specs=in_specs, out_specs=out_specs, check_vma=False
    )
```
